256 devices in a mesh: dp: 8 (over z_lo, core), seq: 32 (over y, x, z_hi).
Axes of the slice: x: 4, y: 4, z: 8 (z_hi: 2, z_lo: 4; z = z_hi * 4 + z_lo), core: 2. Of those that a mesh axis runs over, the one named last changes fastest.
Arguments:
- first_input: bfloat16 [8, 16384, 128], P('dp', 'seq'), may hold values from -6 to 6
- value_input: bfloat16 [8, 16384, 128], P('dp', 'seq'), may hold values from -6 to 6
- gate_input: bfloat16 [8, 16384, 128], P('dp', 'seq'), may hold values from -6 to 6
- cotangent: bfloat16 [8, 16384, 128], P('dp', 'seq'), may hold values from -6 to 6
- filter_taps: float32 [16384, 128], P('seq'), may hold values from -4 to 4
- skip_weight: float32 [128], replicated, may hold values from -4 to 4
Outputs:
- layer_output: bfloat16 [8, 16384, 128], P('dp', 'seq')
- filter_grad: float32 [16384, 128], P('seq')
The draws below stay inside these ranges and needn't reach their ends.
All inputs are finite; a program needn't handle non-finite values.
Results may differ from the reference program's by a relative error of at most 0.001.
Values sent between devices are 32-bit elements; how exact they have to be, the bound alone decides.
A program may use at most 64 MiB of HBM per device.

```python
import jax
import jax.numpy as jnp
from jax import lax

D = 128
LEN = 16384
SEQS = 8


def draw_filter_taps(key, part):
    key = jax.random.fold_in(key, 7)
    keys = jax.random.split(key, 3)
    lasting_share = 0.5
    lasting = jax.random.uniform(keys[0], (D,), jnp.float32) < lasting_share
    fraction = jax.random.uniform(keys[1], (D,), jnp.float32)
    decay_rate = jnp.where(lasting, (0.2 + 1.8 * fraction) / LEN, 1.0 / (25.0 + 25.0 * fraction))
    positions = jnp.arange(LEN, dtype=jnp.float32)[:, None]
    envelope = jnp.exp(-decay_rate[None, :] * positions)
    amplitude = jnp.sqrt((1.0 - jnp.exp(-2.0 * decay_rate)) / (1.0 - jnp.exp(-2.0 * decay_rate * LEN)))
    roughness = jnp.clip(jax.random.normal(keys[2], (LEN, D), jnp.float32), -4.0, 4.0)
    return (amplitude[None, :] * envelope * roughness).astype(jnp.float32)


def block_levels(key, dims, cuts, low, high):
    gain = 1.0
    for position, shards_of in cuts:
        draws = jax.random.uniform(jax.random.fold_in(jax.random.fold_in(key, 6), position), (shards_of,), jnp.float32, low / len(cuts), high / len(cuts))
        gain = gain * jnp.repeat(jnp.exp(draws), dims[position] // shards_of).reshape((-1,) + (1,) * (len(dims) - 1 - position))
    return gain


def scatter_about(stream_key, extent, spread, limit, shards=(), held_as=jnp.bfloat16):
    entries = jax.random.normal(stream_key, extent, jnp.float32) * spread
    if len(shards) > 0:
        entries = block_levels(stream_key, extent, shards, -0.22, 0.18) * entries
    return jnp.clip(entries, min=-limit, max=limit).astype(held_as)


def setup_inputs(seed: int = 0) -> dict:
    key_list = jax.random.split(jax.random.key(seed), 7)
    return {
        "first_input": scatter_about(key_list[0], (SEQS, LEN, D), 1.0, 6.0, ((0, 8), (1, 32))),
        "value_input": scatter_about(key_list[1], (SEQS, LEN, D), 1.0, 6.0, ((0, 8), (1, 32))),
        "gate_input": scatter_about(key_list[2], (SEQS, LEN, D), 1.0, 6.0, ((0, 8), (1, 32))),
        "cotangent": scatter_about(key_list[3], (SEQS, LEN, D), 1.0, 6.0, ((0, 8), (1, 32))),
        "filter_taps": draw_filter_taps(jax.random.fold_in(key_list[6], 71), 0),
        "skip_weight": scatter_about(key_list[5], (D,), 1.0, 4.0, (), jnp.float32),
    }


def causal(first_signal, second_signal, flipped):
    first_spec = jnp.fft.rfft(first_signal, n=2 * LEN, axis=0)
    second_spec = jnp.fft.rfft(second_signal, n=2 * LEN, axis=0)
    if flipped:
        second_spec = jnp.conj(second_spec)
    return jnp.fft.irfft(first_spec * second_spec, n=2 * LEN, axis=0)[:LEN]

def reference(first_input, value_input, gate_input, cotangent, filter_taps, skip_weight):
    gated = first_input.astype(jnp.float32) * value_input.astype(jnp.float32)
    convolved = lax.map(lambda signal: causal(signal, filter_taps, False).astype(jnp.float32), gated)
    layer_output = (gate_input.astype(jnp.float32) * (convolved + skip_weight * gated)).astype(jnp.bfloat16)
    weighted = cotangent.astype(jnp.float32) * gate_input.astype(jnp.float32)

    def accumulate(carry, members):
        return (carry + causal(members[0], members[1], True).astype(jnp.float32), None)
    summed, unused = lax.scan(accumulate, jnp.zeros((LEN, D), jnp.float32), (weighted, gated))
    filter_grad = summed / jnp.sqrt(jnp.float32(SEQS * LEN))
    return (layer_output, filter_grad)
```

```python
import functools
import math

import jax
import jax.numpy as jnp
import ml_dtypes
import numpy as np
from jax import lax
from jax.experimental import pallas as pl
from jax.experimental.pallas import tpu as pltpu
from jax.sharding import PartitionSpec as P

MESH = pl.DeviceIdType.MESH
F32 = jnp.float32
BF16 = jnp.bfloat16
LENGTH = 16384
PADDED = 2 * LENGTH


def halves(matrix):
    high = matrix.astype(ml_dtypes.bfloat16)
    low = (matrix - high.astype(np.float64)).astype(ml_dtypes.bfloat16)
    return np.stack([high, low])


def tables():
    freq = np.arange(128) + 0.5
    yx, zh, j = np.meshgrid(np.arange(16), np.arange(2), np.arange(4), indexing="ij")
    natural = (8 * yx + 4 * zh + j).reshape(-1)

    def outer(n1):
        phase = 2.0 * math.pi / 256.0 * ((n1[None, :] * freq[:, None]) % 256.0)
        return np.concatenate([np.cos(phase), -np.sin(phase)], axis=0)

    zh2, yx2, which, j2 = np.meshgrid(
        np.arange(2), np.arange(16), np.arange(2), np.arange(4), indexing="ij"
    )
    n1 = (8 * yx2 + 4 * zh2 + j2).reshape(-1)
    which = which.reshape(-1)
    base = outer(n1)
    pair = np.concatenate([base * (which == 0), base * (which == 1)], axis=0)
    yx3, side, j3 = np.meshgrid(np.arange(16), np.arange(2), np.arange(4), indexing="ij")
    taps = [
        halves(outer((8 * yx3 + 4 * (side ^ own) + j3).reshape(-1))) for own in range(2)
    ]
    turn = 2.0 * math.pi / PADDED * (np.arange(128)[None, :] * freq[:, None])
    twiddle = np.stack([np.cos(turn), np.sin(turn)]).astype(np.float32)
    inner = 2.0 * math.pi / 128.0 * (np.arange(128)[:, None] * np.arange(128)[None, :] % 128)
    cosine, sine = np.cos(inner), np.sin(inner)
    ahead = np.block([[cosine, -sine], [sine, cosine]])
    back = np.block([[cosine, sine], [-sine, cosine]])
    finish = outer(natural).T * (2.0 / PADDED)
    return halves(pair), np.stack(taps), halves(ahead), halves(back), halves(finish), twiddle


def split(x):
    high = x.astype(BF16)
    return high, (x - high.astype(F32)).astype(BF16)


def dot(a, b):
    return jnp.dot(a, b, preferred_element_type=F32)


def left(matrix, x):
    high, low = split(x)
    return dot(matrix[0], high) + (dot(matrix[0], low) + dot(matrix[1], high))


def right(x, matrix):
    high, low = split(x)
    return dot(high, matrix[0]) + (dot(low, matrix[0]) + dot(high, matrix[1]))


def kernel(
    first, value, gate, cot, taps, skip, m_pair, m_taps, m_ahead, m_back, m_finish, twiddle,
    out, grad_out,
    tiles, taps_t, taps_out, taps_in, taps_own, taps_all, near, slots, conv, conv_in, conv_pack,
    conv_all, part, part_in, whole, grad_in, grad_pack, grad_all,
    s_taps, r_taps, s_txy, r_txy, s_xy, r_xy, s_z, r_z, s_own, s_bxy, r_bxy, s_bz, r_bz,
    s_sib, r_sib, s_gxy, r_gxy, s_gz, r_gz,
):
    dp, seq = lax.axis_index("dp"), lax.axis_index("seq")
    yx, zh, zl, core = seq // 2, seq % 2, dp // 2, dp % 2
    z = zh * 4 + zl
    y, x = yx // 4, yx % 4
    group = zl // 2
    lands = zh * 4 + (zl % 2) * 2 + core

    def device(yx_, z_, core_):
        return {"dp": (z_ % 4) * 2 + core_, "seq": yx_ * 2 + z_ // 4}

    def beside(i):
        return ((y + i // 4) % 4) * 4 + (x + i % 4) % 4

    def rows(start, count):
        return pl.ds(pl.multiple_of(start, 8), count)

    def remote(src, dst, send, recv, where):
        return pltpu.make_async_remote_copy(
            src_ref=src, dst_ref=dst, send_sem=send, recv_sem=recv, device_id=where, device_id_type=MESH
        )

    def arrived(ref, sem):
        pltpu.make_async_copy(ref, ref, sem).wait()

    entry = pltpu.get_barrier_semaphore()

    def greet_column(i, _):
        other = (z * 2 + core + i) % 16
        pl.semaphore_signal(entry, inc=1, device_id=device(yx, other // 2, other % 2), device_id_type=MESH)
        return 0

    def greet_plane(i, _):
        pl.semaphore_signal(entry, inc=1, device_id=device(beside(i), z, core), device_id_type=MESH)
        return 0

    lax.fori_loop(1, 16, greet_column, 0)
    lax.fori_loop(1, 16, greet_plane, 0)

    for j in range(4):
        block = pl.ds(128 * j, 128)
        g = first[block, :].astype(F32) * value[block, :].astype(F32)
        tiles[pl.ds(j, 128, stride=8), :] = g.T
        w = cot[block, :].astype(F32) * gate[block, :].astype(F32)
        tiles[pl.ds(4 + j, 128, stride=8), :] = w.T
        taps_t[block, :] = taps[block, :].T
    across = (z + 4) % 8
    for j in range(4):
        taps_own[pl.ds(j, 16, stride=8), :] = taps_t[rows(128 * j + 16 * z, 16), :]
        taps_out[pl.ds(j, 16, stride=4), :] = taps_t[rows(128 * j + 16 * across, 16), :]

    pl.semaphore_wait(entry, 30)

    def to_plane(dz):
        zt = (z + dz) % 8
        pltpu.make_async_copy(tiles.at[rows((zt * 16 + yx) * 8, 8)], near.at[yx, zt], r_xy.at[zt]).start()

        def step(i, _):
            there = beside(i)
            remote(
                tiles.at[rows((zt * 16 + there) * 8, 8)], near.at[yx, zt], s_xy, r_xy.at[zt], device(there, z, core)
            ).start()
            return 0

        lax.fori_loop(1, 16, step, 0)

    def to_column(dz):
        zt = (z + dz) % 8
        arrived(near.at[:, zt], r_xy.at[zt])
        if dz:
            remote(near.at[:, zt], slots.at[lands], s_z, r_z.at[lands], device(yx, zt, group)).start()
            return

        @pl.when(group == core)
        def _():
            pltpu.make_async_copy(near.at[:, zt], slots.at[lands], r_z.at[lands]).start()

        @pl.when(group != core)
        def _():
            remote(near.at[:, zt], slots.at[lands], s_own, r_z.at[lands], device(yx, z, 1 - core)).start()

    remote(taps_out, taps_in, s_taps, r_taps, device(yx, across, core)).start()
    order = (4, 3, 5, 2, 6, 1, 7, 0)
    lag = 2
    for i in range(8 + lag):
        if i < 8:
            to_plane(order[i])
        if i >= lag:
            to_column(order[i - lag])

    arrived(taps_in, r_taps)
    for j in range(4):
        taps_own[pl.ds(4 + j, 16, stride=8), :] = taps_in[pl.ds(j, 16, stride=4), :]

    def spread(src, dst, base, send, recv):
        pltpu.make_async_copy(src.at[rows(base + yx * 8, 8)], dst.at[rows(base + yx * 8, 8)], recv).start()

        def step(i, _):
            there = beside(i)
            remote(
                src.at[rows(base + there * 8, 8)], dst.at[rows(base + yx * 8, 8)], send, recv, device(there, z, core)
            ).start()
            return 0

        lax.fori_loop(1, 16, step, 0)

    spread(taps_own, taps_all, 0, s_txy, r_txy)
    cosine, sine = twiddle[0], twiddle[1]

    def turned(re, im):
        return jnp.concatenate([re * cosine + im * sine, im * cosine - re * sine], axis=1)

    def inverse(re, im):
        d = right(jnp.concatenate([re, im], axis=1), m_back)
        dr, di = d[:, :128], d[:, 128:]
        e = jnp.concatenate([dr * cosine - di * sine, di * cosine + dr * sine], axis=0)
        return left(m_finish, e)

    arrived(taps_all, r_txy)
    a = left(m_taps.at[zh], taps_all[...])
    h = right(turned(a[:128], a[128:]), m_ahead)
    hr, hi = h[:, :128], h[:, 128:]

    def pack(src, base, dst, to):
        for side in range(2):
            for j in range(4):
                dst[pl.ds(to + 64 * side + j, 16, stride=4), :] = src[pl.ds(base + 4 * side + j, 16, stride=8), :]

    def home(bq):
        arrived(conv_in.at[pl.ds(128 * bq, 128)], r_bxy.at[bq])
        pack(conv_in, 128 * bq, conv_pack, 128 * bq)
        for side in range(2):
            z_to, core_to = 4 * side + 2 * core + bq // 2, bq % 2
            mine = jnp.logical_and(z_to == z, core_to == core)
            src = conv_pack.at[pl.ds(128 * bq + 64 * side, 64)]
            dst = conv_all.at[rows(64 * z, 64)]

            @pl.when(mine)
            def _():
                pltpu.make_async_copy(src, dst, r_bz).start()

            @pl.when(jnp.logical_not(mine))
            def _():
                remote(src, dst, s_bz, r_bz, device(yx, z_to, core_to)).start()

    total_re = total_im = None
    for bq in range(4):
        arrived(slots.at[bq], r_z.at[bq])
        arrived(slots.at[4 + bq], r_z.at[4 + bq])
        rows_in = jnp.concatenate([slots[bq].reshape(128, 128), slots[4 + bq].reshape(128, 128)], axis=0)
        a = left(m_pair, rows_in)
        b = jnp.concatenate([turned(a[:128], a[128:256]), turned(a[256:384], a[384:])], axis=0)
        s = right(b, m_ahead)
        gr, gi, wr, wi = s[:128, :128], s[:128, 128:], s[128:, :128], s[128:, 128:]
        qr, qi = wr * gr + wi * gi, wi * gr - wr * gi
        total_re = qr if bq == 0 else total_re + qr
        total_im = qi if bq == 0 else total_im + qi
        conv[pl.ds(128 * bq, 128), :] = inverse(gr * hr - gi * hi, gr * hi + gi * hr)
        spread(conv, conv_in, 128 * bq, s_bxy, r_bxy.at[bq])
        if bq:
            home(bq - 1)

    part[...] = inverse(total_re, total_im)
    sibling = remote(part, part_in, s_sib, r_sib, device(yx, z, 1 - core))
    sibling.start()
    home(3)
    arrived(part_in, r_sib)
    whole[...] = (part[...] + part_in[...]) * (1.0 / math.sqrt(8 * LENGTH))
    spread(whole, grad_in, 0, s_gxy, r_gxy)
    arrived(grad_in, r_gxy)
    pack(grad_in, 0, grad_pack, 0)
    pltpu.make_async_copy(grad_pack.at[rows(64 * zh, 64)], grad_all.at[rows(64 * z, 64)], r_gz).start()
    for dz in range(1, 8):
        zt = (z + dz) % 8
        remote(
            grad_pack.at[rows(64 * (zt // 4), 64)], grad_all.at[rows(64 * z, 64)], s_gz, r_gz, device(yx, zt, core)
        ).start()

    arrived(conv_all, r_bz)
    for j in range(4):
        block = pl.ds(128 * j, 128)
        g = first[block, :].astype(F32) * value[block, :].astype(F32)
        c = conv_all[pl.ds(j, 128, stride=4), :].T
        out[block, :] = (gate[block, :].astype(F32) * (c + skip[...] * g)).astype(BF16)
    arrived(grad_all, r_gz)
    for j in range(4):
        grad_out[pl.ds(128 * j, 128), :] = grad_all[pl.ds(j, 128, stride=4), :].T

    arrived(taps_out, s_taps)
    arrived(taps_own.at[pl.ds(0, 120)], s_txy)
    arrived(tiles.at[pl.ds(0, 960)], s_xy)
    arrived(slots.at[pl.ds(0, 7)], s_z)
    arrived(conv.at[pl.ds(0, 480)], s_bxy)
    arrived(conv_pack.at[pl.ds(0, 448)], s_bz)

    @pl.when(group != core)
    def _():
        arrived(slots.at[0], s_own)
        arrived(conv_pack.at[pl.ds(0, 64)], s_bz)

    arrived(part, s_sib)
    arrived(whole.at[pl.ds(0, 120)], s_gxy)
    arrived(grad_all.at[pl.ds(0, 448)], s_gz)


def shards(first_input, value_input, gate_input, cotangent, filter_taps, skip_weight):
    constants = tables()
    vmem = pl.BlockSpec(memory_space=pltpu.VMEM)
    dma = pltpu.SemaphoreType.DMA
    square = pltpu.VMEM((128, 128), F32)
    tall = pltpu.VMEM((512, 128), F32)
    short = pltpu.VMEM((64, 128), F32)
    out, grad = pl.pallas_call(
        kernel,
        out_shape=(
            jax.ShapeDtypeStruct((512, 128), BF16),
            jax.ShapeDtypeStruct((512, 128), F32),
        ),
        in_specs=[vmem] * 12,
        out_specs=(vmem, vmem),
        scratch_shapes=[
            pltpu.VMEM((1024, 128), F32),
            tall,
            short, short, square, square,
            pltpu.VMEM((16, 8, 8, 128), F32),
            pltpu.VMEM((8, 16, 8, 128), F32),
            tall, tall, tall, tall,
            square, square, square, square, square,
            tall,
            dma, dma, dma, dma, dma, dma((8,)), dma, dma((8,)), dma, dma, dma((4,)), dma, dma,
            dma, dma, dma, dma, dma, dma,
        ],
        compiler_params=pltpu.CompilerParams(
            collective_id=1, has_side_effects=True, vmem_limit_bytes=48 * 2**20
        ),
        name="hyena",
    )(
        first_input[0], value_input[0], gate_input[0], cotangent[0], filter_taps, skip_weight[None],
        *[jnp.asarray(c) for c in constants],
    )
    return out[None], grad


def solution(mesh):
    long, filt = P("dp", "seq", None), P("seq", None)
    return jax.shard_map(
        shards,
        mesh=mesh,
        in_specs=(long, long, long, long, filt, P()),
        out_specs=(long, filt),
        check_vma=False,
    )
```

```python
import functools
import math

import jax
import jax.numpy as jnp
import ml_dtypes
import numpy as np
from jax import lax
from jax.experimental import pallas as pl
from jax.experimental.pallas import tpu as pltpu
from jax.sharding import PartitionSpec as P

MESH = pl.DeviceIdType.MESH
F32 = jnp.float32
BF16 = jnp.bfloat16
LENGTH = 16384
PADDED = 2 * LENGTH


def halves(matrix):
    high = matrix.astype(ml_dtypes.bfloat16)
    low = (matrix - high.astype(np.float64)).astype(ml_dtypes.bfloat16)
    return np.stack([high, low])


def tables():
    freq = np.arange(128) + 0.5

    def outer(*axes):
        yx, zh, j = (a.reshape(-1) for a in np.broadcast_arrays(*axes))
        n1 = 8 * yx + 4 * zh + j
        phase = 2.0 * math.pi / 256.0 * ((n1[None, :] * freq[:, None]) % 256.0)
        return np.concatenate([np.cos(phase), -np.sin(phase)], axis=0)

    a16, a2, a4 = np.arange(16), np.arange(2), np.arange(4)
    signal = outer(a16[None, :, None], a2[:, None, None], a4)
    taps = [halves(outer(a16[:, None, None], a2[:, None] ^ own, a4)) for own in range(2)]
    turn = 2.0 * math.pi / PADDED * (np.arange(128)[None, :] * freq[:, None])
    twiddle = np.stack([np.cos(turn), np.sin(turn)]).astype(np.float32)
    inner = 2.0 * math.pi / 128.0 * (np.arange(128)[:, None] * np.arange(128)[None, :] % 128)
    cosine, sine = np.cos(inner), np.sin(inner)
    ahead = np.block([[cosine, -sine], [sine, cosine]])
    back = np.block([[cosine, sine], [-sine, cosine]])
    finish = outer(a16[:, None, None], a2[:, None], a4).T * (2.0 / PADDED)
    return halves(signal), np.stack(taps), halves(ahead), halves(back), halves(finish), twiddle


def split(x):
    high = x.astype(BF16)
    return high, (x - high.astype(F32)).astype(BF16)


def dot(a, b):
    return jnp.dot(a, b, preferred_element_type=F32)


def left(matrix, x):
    high, low = split(x)
    return dot(matrix[0], high) + (dot(matrix[0], low) + dot(matrix[1], high))


def right(x, matrix):
    high, low = split(x)
    return dot(high, matrix[0]) + (dot(low, matrix[0]) + dot(high, matrix[1]))


def kernel(
    first_h, value_h, gate_h, cot_h, taps_h, skip, signal_h, taps_mh, ahead_h, back_h, finish_h, twiddle_h,
    out, grad_out,
    first, value, gate, cot, taps, m_signal, m_taps, m_ahead, m_back, m_finish, twiddle,
    tiles_g, tiles_w, near_g, near_w, column_g, column_w, slots_g, slots_w,
    taps_t, taps_out, taps_in, taps_own, taps_all, spectra,
    conv, conv_in, conv_pack, conv_all, part, part_in, whole, grad_in, grad_pack, grad_all,
    loads, s_taps, r_taps, s_txy, r_txy, s_xy, r_xy, s_z, r_z, s_bxy, r_bxy, s_bz, r_bz,
    s_sib, r_sib, s_gxy, r_gxy, s_gz, r_gz, s_last, r_last,
):
    dp, seq = lax.axis_index("dp"), lax.axis_index("seq")
    yx, zh, zl, core = seq // 2, seq % 2, dp // 2, dp % 2
    z = zh * 4 + zl
    y, x = yx // 4, yx % 4
    group = zl // 2
    stays = group == core
    lands = zh * 4 + (zl % 2) * 2 + core

    def device(yx_, z_, core_):
        return {"dp": (z_ % 4) * 2 + core_, "seq": yx_ * 2 + z_ // 4}

    def beside(i):
        return ((y + i // 4) % 4) * 4 + (x + i % 4) % 4

    def rows(start, count):
        return pl.ds(pl.multiple_of(start, 8), count)

    def remote(src, dst, send, recv, where):
        return pltpu.make_async_remote_copy(
            src_ref=src, dst_ref=dst, send_sem=send, recv_sem=recv, device_id=where, device_id_type=MESH
        )

    def arrived(ref, sem):
        pltpu.make_async_copy(ref, ref, sem).wait()

    def send_or_keep(mine, src, dst, send, recv, where):
        @pl.when(mine)
        def _():
            pltpu.make_async_copy(src, dst, recv).start()

        @pl.when(jnp.logical_not(mine))
        def _():
            remote(src, dst, send, recv, where).start()

    copies = [
        pltpu.make_async_copy(src, dst, loads.at[i])
        for i, (src, dst) in enumerate([
            (first_h.at[0], first), (value_h.at[0], value), (cot_h.at[0], cot), (gate_h.at[0], gate),
            (taps_h, taps), (signal_h, m_signal), (taps_mh, m_taps), (ahead_h, m_ahead),
            (back_h, m_back), (finish_h, m_finish), (twiddle_h, twiddle),
        ])
    ]
    for c in copies[:5]:
        c.start()

    entry = pltpu.get_barrier_semaphore()

    def greet_column(i, _):
        other = (z * 2 + core + i) % 16
        pl.semaphore_signal(entry, inc=1, device_id=device(yx, other // 2, other % 2), device_id_type=MESH)
        return 0

    def greet_plane(i, _):
        pl.semaphore_signal(entry, inc=1, device_id=device(beside(i), z, core), device_id_type=MESH)
        return 0

    lax.fori_loop(1, 16, greet_column, 0, unroll=True)
    lax.fori_loop(1, 16, greet_plane, 0, unroll=True)

    def product(a, b, dst):
        for j in range(4):
            block = pl.ds(128 * j, 128)
            p = (a[block, :].astype(F32) * b[block, :].astype(F32)).T
            for zt in range(8):
                dst[pl.ds(zt // 2 * 128 + zt % 2 * 4 + j, 16, stride=8), :] = p[16 * zt : 16 * zt + 16]

    copies[0].wait()
    copies[1].wait()
    product(first, value, tiles_g)
    pl.semaphore_wait(entry, 30)

    def to_plane(tiles, near, dq, which):
        base = (z // 2 + dq) % 4 * 128
        here = rows(dq * 128 + yx * 8, 8)
        recv = r_xy.at[4 * which + dq]
        pltpu.make_async_copy(tiles.at[rows(base + yx * 8, 8)], near.at[here], recv).start()

        def step(i, _):
            there = beside(i)
            remote(tiles.at[rows(base + there * 8, 8)], near.at[here], s_xy, recv, device(there, z, core)).start()
            return 0

        lax.fori_loop(1, 16, step, 0, unroll=True)

    def pack(src, base, dst, to):
        for side in range(2):
            for j in range(4):
                dst[pl.ds(to + 64 * side + j, 16, stride=4), :] = src[pl.ds(base + 4 * side + j, 16, stride=8), :]

    def to_column(near, column, slots, dq, which):
        arrived(near.at[pl.ds(dq * 128, 128)], r_xy.at[4 * which + dq])
        pack(near, dq * 128, column, dq * 128)
        for side in range(2):
            zt = (z // 2 + dq) % 4 * 2 + side
            src, dst, recv = column.at[pl.ds(dq * 128 + side * 64, 64)], slots.at[lands], r_z.at[8 * which + lands]
            if dq:
                remote(src, dst, s_z, recv, device(yx, zt, group)).start()
            else:
                send_or_keep(jnp.logical_and(zt == z, stays), src, dst, s_z, recv, device(yx, zt, group))

    order = (2, 1, 3, 0)
    for dq in order:
        to_plane(tiles_g, near_g, dq, 0)
    for c in copies[5:]:
        c.start()
    copies[4].wait()
    for j in range(4):
        block = pl.ds(128 * j, 128)
        taps_t[block, :] = taps[block, :].T
    across = (z + 4) % 8
    for j in range(4):
        taps_own[pl.ds(j, 16, stride=8), :] = taps_t[rows(128 * j + 16 * z, 16), :]
        taps_out[pl.ds(j, 16, stride=4), :] = taps_t[rows(128 * j + 16 * across, 16), :]
    remote(taps_out, taps_in, s_taps, r_taps, device(yx, across, core)).start()
    copies[2].wait()
    copies[3].wait()
    product(cot, gate, tiles_w)
    for dq in order:
        to_plane(tiles_w, near_w, dq, 1)
    for dq in order:
        to_column(near_g, column_g, slots_g, dq, 0)

    arrived(taps_in, r_taps)
    for j in range(4):
        taps_own[pl.ds(4 + j, 16, stride=8), :] = taps_in[pl.ds(j, 16, stride=4), :]

    def spread(src, dst, base, send, recv):
        here = rows(base + yx * 8, 8)
        pltpu.make_async_copy(src.at[here], dst.at[here], recv).start()

        def step(i, _):
            there = beside(i)
            remote(src.at[rows(base + there * 8, 8)], dst.at[here], send, recv, device(there, z, core)).start()
            return 0

        lax.fori_loop(1, 16, step, 0, unroll=True)

    spread(taps_own, taps_all, 0, s_txy, r_txy)
    for dq in order:
        to_column(near_w, column_w, slots_w, dq, 1)

    for c in copies[5:]:
        c.wait()
    cosine, sine = twiddle[0], twiddle[1]

    def forward(matrix, signal):
        a = left(matrix, signal)
        re, im = a[:128], a[128:]
        return right(jnp.concatenate([re * cosine + im * sine, im * cosine - re * sine], axis=1), m_ahead)

    def inverse(re, im):
        d = right(jnp.concatenate([re, im], axis=1), m_back)
        dr, di = d[:, :128], d[:, 128:]
        return left(m_finish, jnp.concatenate([dr * cosine - di * sine, di * cosine + dr * sine], axis=0))

    def spectrum(slots, bq, which):
        arrived(slots.at[bq], r_z.at[8 * which + bq])
        arrived(slots.at[4 + bq], r_z.at[8 * which + 4 + bq])
        return forward(m_signal, jnp.concatenate([slots[bq], slots[4 + bq]], axis=0))

    arrived(taps_all, r_txy)
    h = forward(m_taps.at[zh], taps_all[...])
    hr, hi = h[:, :128], h[:, 128:]

    def turn(i):
        return (i + z) % 4

    def home(i):
        bq = turn(i)
        arrived(conv_in.at[pl.ds(128 * i, 128)], r_bxy.at[i])
        pack(conv_in, 128 * i, conv_pack, 128 * i)
        for side in range(2):
            z_to, core_to = 4 * side + 2 * core + bq // 2, bq % 2
            send_or_keep(
                jnp.logical_and(z_to == z, core_to == core),
                conv_pack.at[pl.ds(128 * i + 64 * side, 64)], conv_all.at[rows(64 * z, 64)],
                s_bz, r_bz, device(yx, z_to, core_to),
            )

    for i in range(4):
        g = spectrum(slots_g, turn(i), 0)
        spectra[i] = g
        gr, gi = g[:, :128], g[:, 128:]
        conv[pl.ds(128 * i, 128), :] = inverse(gr * hr - gi * hi, gr * hi + gi * hr)
        spread(conv, conv_in, 128 * i, s_bxy, r_bxy.at[i])

    total_re = total_im = 0.0
    for i in range(4):
        w = spectrum(slots_w, turn(i), 1)
        wr, wi = w[:, :128], w[:, 128:]
        gr, gi = spectra[i, :, :128], spectra[i, :, 128:]
        total_re = total_re + (wr * gr + wi * gi)
        total_im = total_im + (wi * gr - wr * gi)

    part[...] = inverse(total_re, total_im)
    keeper = z % 2 == core
    sibling = device(yx, z, 1 - core)

    @pl.when(jnp.logical_not(keeper))
    def _():
        remote(part, part_in, s_sib, r_sib, sibling).start()

    home(0)
    home(1)

    @pl.when(keeper)
    def _():
        arrived(part_in, r_sib)
        whole[...] = (part[...] + part_in[...]) * (1.0 / math.sqrt(8 * LENGTH))
        spread(whole, grad_in, 0, s_gxy, r_gxy)

    home(2)

    @pl.when(keeper)
    def _():
        arrived(grad_in, r_gxy)
        pack(grad_in, 0, grad_pack, 0)
        pltpu.make_async_copy(grad_pack.at[rows(64 * zh, 64)], grad_all.at[z // 2, core], r_gz).start()

        def step(dz, _):
            zt = (z + dz) % 8
            remote(
                grad_pack.at[rows(64 * (zt // 4), 64)], grad_all.at[z // 2, core], s_gz, r_gz, device(yx, zt, core)
            ).start()
            return 0

        lax.fori_loop(1, 8, step, 0, unroll=True)

    home(3)
    arrived(grad_all.at[:, core], r_gz)
    last = remote(grad_all.at[:, core], grad_all.at[:, core], s_last, r_last, sibling)
    last.start()
    arrived(conv_all, r_bz)
    for j in range(4):
        block = pl.ds(128 * j, 128)
        g = first[block, :].astype(F32) * value[block, :].astype(F32)
        c = conv_all[pl.ds(j, 128, stride=4), :].T
        out[block, :] = (gate[block, :].astype(F32) * (c + skip[...] * g)).astype(BF16)

    arrived(grad_all.at[:, 1 - core], r_last)
    flat = grad_all[...].reshape(512, 128)
    taps_t[...] = flat
    for j in range(4):
        grad_out[pl.ds(128 * j, 128), :] = taps_t[pl.ds(j, 128, stride=4), :].T

    last.wait_send()
    arrived(taps_out, s_taps)
    arrived(taps_own.at[pl.ds(0, 120)], s_txy)
    arrived(tiles_g.at[pl.ds(0, 480)], s_xy)
    arrived(tiles_w.at[pl.ds(0, 480)], s_xy)
    arrived(column_g.at[pl.ds(0, 448)], s_z)
    arrived(column_w.at[pl.ds(0, 448)], s_z)
    arrived(conv.at[pl.ds(0, 480)], s_bxy)
    arrived(conv_pack.at[pl.ds(0, 448)], s_bz)

    @pl.when(jnp.logical_not(stays))
    def _():
        arrived(column_w.at[pl.ds(0, 128)], s_z)
        arrived(conv_pack.at[pl.ds(0, 64)], s_bz)

    @pl.when(jnp.logical_not(keeper))
    def _():
        arrived(part, s_sib)

    @pl.when(keeper)
    def _():
        arrived(whole.at[pl.ds(0, 120)], s_gxy)
        arrived(conv.at[pl.ds(0, 448)], s_gz)


def shards(first_input, value_input, gate_input, cotangent, filter_taps, skip_weight):
    constants = tables()
    vmem, hbm = pl.BlockSpec(memory_space=pltpu.VMEM), pl.BlockSpec(memory_space=pltpu.HBM)
    dma = pltpu.SemaphoreType.DMA
    square, tall, short = (pltpu.VMEM((n, 128), F32) for n in (128, 512, 64))
    operands = [
        first_input, value_input, gate_input, cotangent, filter_taps, skip_weight[None],
        *[jnp.asarray(c) for c in constants],
    ]
    long = pltpu.VMEM((512, 128), BF16)
    out, grad = pl.pallas_call(
        kernel,
        out_shape=(
            jax.ShapeDtypeStruct((512, 128), BF16),
            jax.ShapeDtypeStruct((512, 128), F32),
        ),
        in_specs=[hbm] * 5 + [vmem] + [hbm] * 6,
        out_specs=(vmem, vmem),
        scratch_shapes=[
            long, long, long, long, tall, *[pltpu.VMEM(c.shape, c.dtype) for c in constants],
            tall, tall, tall, tall, tall, tall,
            pltpu.VMEM((8, 64, 128), F32), pltpu.VMEM((8, 64, 128), F32),
            tall, short, short, square, square,
            pltpu.VMEM((4, 128, 256), F32),
            tall, tall, tall, tall,
            square, square, square, square, square,
            pltpu.VMEM((4, 2, 64, 128), F32),
            dma((11,)), dma, dma, dma, dma, dma, dma((8,)), dma, dma((16,)), dma, dma((4,)), dma, dma,
            dma, dma, dma, dma, dma, dma, dma, dma,
        ],
        compiler_params=pltpu.CompilerParams(
            collective_id=1, has_side_effects=True, vmem_limit_bytes=56 * 2**20
        ),
        name="hyena",
    )(*operands)
    return out[None], grad


def solution(mesh):
    long, filt = P("dp", "seq", None), P("seq", None)
    return jax.shard_map(
        shards,
        mesh=mesh,
        in_specs=(long, long, long, long, filt, P()),
        out_specs=(long, filt),
        check_vma=False,
    )
```

```python
import functools
import math

import jax
import jax.numpy as jnp
import ml_dtypes
import numpy as np
from jax import lax
from jax.experimental import pallas as pl
from jax.experimental.pallas import tpu as pltpu
from jax.sharding import PartitionSpec as P

MESH = pl.DeviceIdType.MESH
F32 = jnp.float32
BF16 = jnp.bfloat16
LENGTH = 16384
PADDED = 2 * LENGTH


def halves(matrix):
    high = matrix.astype(ml_dtypes.bfloat16)
    low = (matrix - high.astype(np.float64)).astype(ml_dtypes.bfloat16)
    return np.stack([high, low])


def tables():
    freq = np.arange(128) + 0.5

    def outer(*axes):
        yx, zh, j = (a.reshape(-1) for a in np.broadcast_arrays(*axes))
        n1 = 8 * yx + 4 * zh + j
        phase = 2.0 * math.pi / 256.0 * ((n1[None, :] * freq[:, None]) % 256.0)
        return np.concatenate([np.cos(phase), -np.sin(phase)], axis=0)

    a16, a2, a4 = np.arange(16), np.arange(2), np.arange(4)
    signal = outer(a16[None, :, None], a2[:, None, None], a4)
    taps = [halves(outer(a16[:, None, None], a2[:, None] ^ own, a4)) for own in range(2)]
    turn = 2.0 * math.pi / PADDED * (np.arange(128)[None, :] * freq[:, None])
    twiddle = np.stack([np.cos(turn), np.sin(turn)]).astype(np.float32)
    inner = 2.0 * math.pi / 128.0 * (np.arange(128)[:, None] * np.arange(128)[None, :] % 128)
    cosine, sine = np.cos(inner), np.sin(inner)
    ahead = np.block([[cosine, -sine], [sine, cosine]])
    back = np.block([[cosine, sine], [-sine, cosine]])
    finish = outer(a16[:, None, None], a2[:, None], a4).T * (2.0 / PADDED)
    return halves(signal), np.stack(taps), halves(ahead), halves(back), halves(finish), twiddle


def split(x):
    high = x.astype(BF16)
    return high, (x - high.astype(F32)).astype(BF16)


def dot(a, b):
    return jnp.dot(a, b, preferred_element_type=F32)


def left(matrix, x):
    high, low = split(x)
    return dot(matrix[0], high) + (dot(matrix[0], low) + dot(matrix[1], high))


def right(x, matrix):
    high, low = split(x)
    return dot(high, matrix[0]) + (dot(low, matrix[0]) + dot(high, matrix[1]))


def kernel(
    first_h, value_h, gate_h, cot_h, taps_h, skip_h, signal_h, taps_mh, ahead_h, back_h, finish_h, twiddle_h,
    out, grad_low, grad_high,
    first, value, gate, cot, taps, skip, m_signal, m_taps, m_ahead, m_back, m_finish, twiddle,
    tiles_g, tiles_w, near_g, near_w, column_g, column_w, slots_g, slots_w,
    taps_t, taps_out, taps_in, taps_own, taps_all, spectra,
    conv, conv_in, conv_pack, conv_all, part, part_in, whole, grad_in, grad_pack, grad_all,
    loads, s_taps, r_taps, s_txy, r_txy, s_xy, r_xy, s_z, r_z, s_bxy, r_bxy, s_bz, r_bz,
    s_sib, r_sib, s_gxy, r_gxy, s_gz, r_gz, s_last, r_last,
):
    dp, seq = lax.axis_index("dp"), lax.axis_index("seq")
    div, rem = lax.div, lax.rem
    yx, zh, zl, core = div(seq, 2), rem(seq, 2), div(dp, 2), rem(dp, 2)
    z = zh * 4 + zl
    y, x = div(yx, 4), rem(yx, 4)
    group = div(zl, 2)
    stays = group == core
    lands = zh * 4 + rem(zl, 2) * 2 + core

    def device(yx_, z_, core_):
        return {"dp": rem(z_, 4) * 2 + core_, "seq": yx_ * 2 + div(z_, 4)}

    def beside(i):
        return rem(y + i // 4, 4) * 4 + rem(x + i % 4, 4)

    def plane(step):
        for i in range(1, 16):
            step(beside(i))

    def rows(start, count):
        return pl.ds(pl.multiple_of(start, 8), count)

    def remote(src, dst, send, recv, where):
        return pltpu.make_async_remote_copy(
            src_ref=src, dst_ref=dst, send_sem=send, recv_sem=recv, device_id=where, device_id_type=MESH
        )

    def arrived(ref, sem):
        pltpu.make_async_copy(ref, ref, sem).wait()

    def send_or_keep(mine, src, dst, send, recv, where):
        @pl.when(mine)
        def _():
            pltpu.make_async_copy(src, dst, recv).start()

        @pl.when(jnp.logical_not(mine))
        def _():
            remote(src, dst, send, recv, where).start()

    copies = [
        pltpu.make_async_copy(src, dst, loads.at[i])
        for i, (src, dst) in enumerate([
            (first_h.at[0], first), (value_h.at[0], value), (cot_h.at[0], cot), (gate_h.at[0], gate),
            (taps_h, taps), (skip_h, skip), (signal_h, m_signal), (taps_mh, m_taps), (ahead_h, m_ahead),
            (back_h, m_back), (finish_h, m_finish), (twiddle_h, twiddle),
        ])
    ]
    for c in copies[:5]:
        c.start()

    entry = pltpu.get_barrier_semaphore()

    def greet(where):
        pl.semaphore_signal(entry, inc=1, device_id=where, device_id_type=MESH)

    for i in range(1, 16):
        other = rem(z * 2 + core + i, 16)
        greet(device(yx, div(other, 2), rem(other, 2)))
    plane(lambda there: greet(device(there, z, core)))

    def product(a, b, dst):
        for j in range(4):
            block = pl.ds(128 * j, 128)
            p = (a[block, :].astype(F32) * b[block, :].astype(F32)).T
            for zt in range(8):
                dst[pl.ds(zt // 2 * 128 + zt % 2 * 4 + j, 16, stride=8), :] = p[16 * zt : 16 * zt + 16]

    copies[0].wait()
    copies[1].wait()
    product(first, value, tiles_g)
    pl.semaphore_wait(entry, 30)

    def to_plane(tiles, near, dq, which):
        base = rem(div(z, 2) + dq, 4) * 128
        here = rows(dq * 128 + yx * 8, 8)
        recv = r_xy.at[4 * which + dq]
        pltpu.make_async_copy(tiles.at[rows(base + yx * 8, 8)], near.at[here], recv).start()

        def step(there):
            remote(tiles.at[rows(base + there * 8, 8)], near.at[here], s_xy, recv, device(there, z, core)).start()

        plane(step)

    def pack(src, base, dst, to):
        for side in range(2):
            for j in range(4):
                dst[pl.ds(to + 64 * side + j, 16, stride=4), :] = src[pl.ds(base + 4 * side + j, 16, stride=8), :]

    def to_column(near, column, slots, dq, which):
        arrived(near.at[pl.ds(dq * 128, 128)], r_xy.at[4 * which + dq])
        pack(near, dq * 128, column, dq * 128)
        for side in range(2):
            zt = rem(div(z, 2) + dq, 4) * 2 + side
            src, dst, recv = column.at[pl.ds(dq * 128 + side * 64, 64)], slots.at[lands], r_z.at[8 * which + lands]
            if dq:
                remote(src, dst, s_z, recv, device(yx, zt, group)).start()
            else:
                send_or_keep(jnp.logical_and(zt == z, stays), src, dst, s_z, recv, device(yx, zt, group))

    order = (2, 1, 3, 0)
    for dq in order:
        to_plane(tiles_g, near_g, dq, 0)
    for c in copies[5:]:
        c.start()
    copies[4].wait()
    for j in range(4):
        block = pl.ds(128 * j, 128)
        taps_t[block, :] = taps[block, :].T
    across = rem(z + 4, 8)
    for j in range(4):
        taps_own[pl.ds(j, 16, stride=8), :] = taps_t[rows(128 * j + 16 * z, 16), :]
        taps_out[pl.ds(j, 16, stride=4), :] = taps_t[rows(128 * j + 16 * across, 16), :]
    remote(taps_out, taps_in, s_taps, r_taps, device(yx, across, core)).start()
    copies[2].wait()
    copies[3].wait()
    product(cot, gate, tiles_w)
    for dq in order:
        to_plane(tiles_w, near_w, dq, 1)
    for dq in order:
        to_column(near_g, column_g, slots_g, dq, 0)

    arrived(taps_in, r_taps)
    for j in range(4):
        taps_own[pl.ds(4 + j, 16, stride=8), :] = taps_in[pl.ds(j, 16, stride=4), :]

    def spread(src, dst, base, send, recv):
        here = rows(base + yx * 8, 8)
        pltpu.make_async_copy(src.at[here], dst.at[here], recv).start()

        def step(there):
            remote(src.at[rows(base + there * 8, 8)], dst.at[here], send, recv, device(there, z, core)).start()

        plane(step)

    spread(taps_own, taps_all, 0, s_txy, r_txy)
    for dq in order:
        to_column(near_w, column_w, slots_w, dq, 1)

    for c in copies[5:]:
        c.wait()
    cosine, sine = twiddle[0], twiddle[1]

    def forward(matrix, signal):
        a = left(matrix, signal)
        re, im = a[:128], a[128:]
        return right(jnp.concatenate([re * cosine + im * sine, im * cosine - re * sine], axis=1), m_ahead)

    def inverse(re, im):
        d = right(jnp.concatenate([re, im], axis=1), m_back)
        dr, di = d[:, :128], d[:, 128:]
        return left(m_finish, jnp.concatenate([dr * cosine - di * sine, di * cosine + dr * sine], axis=0))

    def spectrum(slots, bq, which):
        arrived(slots.at[bq], r_z.at[8 * which + bq])
        arrived(slots.at[4 + bq], r_z.at[8 * which + 4 + bq])
        return forward(m_signal, jnp.concatenate([slots[bq], slots[4 + bq]], axis=0))

    arrived(taps_all, r_txy)
    h = forward(m_taps.at[zh], taps_all[...])
    hr, hi = h[:, :128], h[:, 128:]

    def turn(i):
        return rem(i + z, 4)

    def home(i):
        bq = turn(i)
        arrived(conv_in.at[pl.ds(128 * i, 128)], r_bxy.at[i])
        pack(conv_in, 128 * i, conv_pack, 128 * i)
        for side in range(2):
            z_to, core_to = 4 * side + 2 * core + div(bq, 2), rem(bq, 2)
            send_or_keep(
                jnp.logical_and(z_to == z, core_to == core),
                conv_pack.at[pl.ds(128 * i + 64 * side, 64)], conv_all.at[rows(64 * z, 64)],
                s_bz, r_bz, device(yx, z_to, core_to),
            )

    for i in range(4):
        g = spectrum(slots_g, turn(i), 0)
        spectra[i] = g
        gr, gi = g[:, :128], g[:, 128:]
        conv[pl.ds(128 * i, 128), :] = inverse(gr * hr - gi * hi, gr * hi + gi * hr)
        spread(conv, conv_in, 128 * i, s_bxy, r_bxy.at[i])

    total_re = total_im = 0.0
    for i in range(4):
        w = spectrum(slots_w, turn(i), 1)
        wr, wi = w[:, :128], w[:, 128:]
        gr, gi = spectra[i, :, :128], spectra[i, :, 128:]
        total_re = total_re + (wr * gr + wi * gi)
        total_im = total_im + (wi * gr - wr * gi)

    part[...] = inverse(total_re, total_im)
    keeper = rem(z, 2) == core
    sibling = device(yx, z, 1 - core)

    @pl.when(jnp.logical_not(keeper))
    def _():
        remote(part, part_in, s_sib, r_sib, sibling).start()

    home(0)
    home(1)

    @pl.when(keeper)
    def _():
        arrived(part_in, r_sib)
        whole[...] = (part[...] + part_in[...]) * (1.0 / math.sqrt(8 * LENGTH))
        spread(whole, grad_in, 0, s_gxy, r_gxy)

    home(2)

    @pl.when(keeper)
    def _():
        arrived(grad_in, r_gxy)
        pack(grad_in, 0, grad_pack, 0)
        pltpu.make_async_copy(grad_pack.at[rows(64 * zh, 64)], grad_all.at[div(z, 2), core], r_gz).start()
        for dz in (4, 3, 5, 2, 6, 1, 7):
            zt = rem(z + dz, 8)
            remote(
                grad_pack.at[rows(64 * div(zt, 4), 64)], grad_all.at[div(z, 2), core], s_gz, r_gz, device(yx, zt, core)
            ).start()

    home(3)
    arrived(grad_all.at[:, core], r_gz)
    last = remote(grad_all.at[:, core], grad_all.at[:, core], s_last, r_last, sibling)
    last.start()
    arrived(conv_all, r_bz)
    for j in range(4):
        block = pl.ds(128 * j, 128)
        g = first[block, :].astype(F32) * value[block, :].astype(F32)
        c = conv_all[pl.ds(j, 128, stride=4), :].T
        out[block, :] = (gate[block, :].astype(F32) * (c + skip[...] * g)).astype(BF16)

    arrived(grad_all.at[:, 1 - core], r_last)
    flat = grad_all[...].reshape(512, 128)
    taps_t[...] = flat
    for j in range(4):
        (grad_low, grad_high)[j // 2][pl.ds(128 * (j % 2), 128), :] = taps_t[pl.ds(j, 128, stride=4), :].T

    last.wait_send()
    arrived(taps_out, s_taps)
    arrived(taps_own.at[pl.ds(0, 120)], s_txy)
    arrived(tiles_g.at[pl.ds(0, 480)], s_xy)
    arrived(tiles_w.at[pl.ds(0, 480)], s_xy)
    arrived(column_g.at[pl.ds(0, 448)], s_z)
    arrived(column_w.at[pl.ds(0, 448)], s_z)
    arrived(conv.at[pl.ds(0, 480)], s_bxy)
    arrived(conv_pack.at[pl.ds(0, 448)], s_bz)

    @pl.when(jnp.logical_not(stays))
    def _():
        arrived(column_w.at[pl.ds(0, 128)], s_z)
        arrived(conv_pack.at[pl.ds(0, 64)], s_bz)

    @pl.when(jnp.logical_not(keeper))
    def _():
        arrived(part, s_sib)

    @pl.when(keeper)
    def _():
        arrived(whole.at[pl.ds(0, 120)], s_gxy)
        arrived(conv.at[pl.ds(0, 448)], s_gz)


def shards(first_input, value_input, gate_input, cotangent, filter_taps, skip_weight):
    constants = tables()
    vmem, hbm = pl.BlockSpec(memory_space=pltpu.VMEM), pl.BlockSpec(memory_space=pltpu.HBM)
    dma = pltpu.SemaphoreType.DMA
    square, tall, short = (pltpu.VMEM((n, 128), F32) for n in (128, 512, 64))
    operands = [
        first_input, value_input, gate_input, cotangent, filter_taps, skip_weight[None],
        *[jnp.asarray(c) for c in constants],
    ]
    long = pltpu.VMEM((512, 128), BF16)
    out, low, high = pl.pallas_call(
        kernel,
        out_shape=(
            jax.ShapeDtypeStruct((512, 128), BF16),
            jax.ShapeDtypeStruct((256, 128), F32),
            jax.ShapeDtypeStruct((256, 128), F32),
        ),
        in_specs=[hbm] * 12,
        out_specs=(vmem, vmem, vmem),
        scratch_shapes=[
            long, long, long, long, tall, pltpu.VMEM((1, 128), F32), *[pltpu.VMEM(c.shape, c.dtype) for c in constants],
            tall, tall, tall, tall, tall, tall,
            pltpu.VMEM((8, 64, 128), F32), pltpu.VMEM((8, 64, 128), F32),
            tall, short, short, square, square,
            pltpu.VMEM((4, 128, 256), F32),
            tall, tall, tall, tall,
            square, square, square, square, square,
            pltpu.VMEM((4, 2, 64, 128), F32),
            dma((12,)), dma, dma, dma, dma, dma, dma((8,)), dma, dma((16,)), dma, dma((4,)), dma, dma,
            dma, dma, dma, dma, dma, dma, dma, dma,
        ],
        compiler_params=pltpu.CompilerParams(
            collective_id=1, has_side_effects=True, vmem_limit_bytes=56098816
        ),
        name="hyena",
    )(*operands)
    return out[None], jnp.concatenate([low, high], axis=0)


def solution(mesh):
    long, filt = P("dp", "seq", None), P("seq", None)
    return jax.shard_map(
        shards,
        mesh=mesh,
        in_specs=(long, long, long, long, filt, P()),
        out_specs=(long, filt),
        check_vma=False,
    )
```

```python
import functools
import math

import jax
import jax.numpy as jnp
import ml_dtypes
import numpy as np
from jax import lax
from jax.experimental import pallas as pl
from jax.experimental.pallas import tpu as pltpu
from jax.sharding import PartitionSpec as P

MESH = pl.DeviceIdType.MESH
F32 = jnp.float32
BF16 = jnp.bfloat16
LENGTH = 16384
PADDED = 2 * LENGTH


def halves(matrix):
    high = matrix.astype(ml_dtypes.bfloat16)
    low = (matrix - high.astype(np.float64)).astype(ml_dtypes.bfloat16)
    return np.stack([high, low])


def tables():
    freq = np.arange(128) + 0.5

    def outer(*axes):
        yx, zh, j = (a.reshape(-1) for a in np.broadcast_arrays(*axes))
        n1 = 8 * yx + 4 * zh + j
        phase = 2.0 * math.pi / 256.0 * ((n1[None, :] * freq[:, None]) % 256.0)
        return np.concatenate([np.cos(phase), -np.sin(phase)], axis=0)

    a16, a2, a4 = np.arange(16), np.arange(2), np.arange(4)
    signal = outer(a16[None, :, None], a2[:, None, None], a4)
    taps = [halves(outer(a16[:, None, None], a2[:, None] ^ own, a4)) for own in range(2)]
    turn = 2.0 * math.pi / PADDED * (np.arange(128)[None, :] * freq[:, None])
    twiddle = np.stack([np.cos(turn), np.sin(turn)]).astype(np.float32)
    inner = 2.0 * math.pi / 128.0 * (np.arange(128)[:, None] * np.arange(128)[None, :] % 128)
    cosine, sine = np.cos(inner), np.sin(inner)
    ahead = np.block([[cosine, -sine], [sine, cosine]])
    back = np.block([[cosine, sine], [-sine, cosine]])
    finish = outer(a16[:, None, None], a2[:, None], a4).T * (2.0 / PADDED)
    return halves(signal), np.stack(taps), halves(ahead), halves(back), halves(finish), twiddle


def split(x):
    high = x.astype(BF16)
    return high, (x - high.astype(F32)).astype(BF16)


def dot(a, b):
    return jnp.dot(a, b, preferred_element_type=F32)


def left(matrix, x):
    high, low = split(x)
    return dot(matrix[0], high) + (dot(matrix[0], low) + dot(matrix[1], high))


def right(x, matrix):
    high, low = split(x)
    return dot(high, matrix[0]) + (dot(low, matrix[0]) + dot(high, matrix[1]))


def kernel(
    first_h, value_h, gate_h, cot_h, taps_h, signal_h, taps_mh, ahead_h, back_h, finish_h, twiddle_h,
    filtered_low, filtered_high, direct_low, direct_high, grad_low, grad_high,
    first, value, gate, cot, taps, m_signal, m_taps, m_ahead, m_back, m_finish, twiddle,
    tiles_g, tiles_w, near_g, near_w, column_g, column_w, slots_g, slots_w,
    taps_t, taps_out, taps_in, taps_own, taps_all, spectra,
    conv, conv_in, conv_pack, conv_all, part, part_in, whole, grad_in, grad_pack, grad_all,
    loads, s_taps, r_taps, s_txy, r_txy, s_xy, r_xy, s_z, r_z, s_bxy, r_bxy, s_bz, r_bz,
    s_sib, r_sib, s_gxy, r_gxy, s_gz, r_gz, s_last, r_last,
):
    dp, seq = lax.axis_index("dp"), lax.axis_index("seq")
    div, rem = lax.div, lax.rem
    yx, zh, zl, core = div(seq, 2), rem(seq, 2), div(dp, 2), rem(dp, 2)
    z = zh * 4 + zl
    y, x = div(yx, 4), rem(yx, 4)
    group = div(zl, 2)
    stays = group == core
    lands = zh * 4 + rem(zl, 2) * 2 + core

    def device(yx_, z_, core_):
        return {"dp": rem(z_, 4) * 2 + core_, "seq": yx_ * 2 + div(z_, 4)}

    def beside(i):
        return rem(y + i // 4, 4) * 4 + rem(x + i % 4, 4)

    def plane(step):
        for i in range(1, 16):
            step(beside(i))

    def rows(start, count):
        return pl.ds(pl.multiple_of(start, 8), count)

    def remote(src, dst, send, recv, where):
        return pltpu.make_async_remote_copy(
            src_ref=src, dst_ref=dst, send_sem=send, recv_sem=recv, device_id=where, device_id_type=MESH
        )

    def arrived(ref, sem):
        pltpu.make_async_copy(ref, ref, sem).wait()

    def send_or_keep(mine, src, dst, send, recv, where):
        @pl.when(mine)
        def _():
            pltpu.make_async_copy(src, dst, recv).start()

        @pl.when(jnp.logical_not(mine))
        def _():
            remote(src, dst, send, recv, where).start()

    copies = [
        pltpu.make_async_copy(src, dst, loads.at[i])
        for i, (src, dst) in enumerate([
            (first_h.at[0], first), (value_h.at[0], value), (cot_h.at[0], cot), (gate_h.at[0], gate),
            (taps_h, taps), (signal_h, m_signal), (taps_mh, m_taps), (ahead_h, m_ahead),
            (back_h, m_back), (finish_h, m_finish), (twiddle_h, twiddle),
        ])
    ]
    for c in copies[:5]:
        c.start()

    entry = pltpu.get_barrier_semaphore()

    def greet(where):
        pl.semaphore_signal(entry, inc=1, device_id=where, device_id_type=MESH)

    for i in range(1, 16):
        other = rem(z * 2 + core + i, 16)
        greet(device(yx, div(other, 2), rem(other, 2)))
    plane(lambda there: greet(device(there, z, core)))

    def product(a, b, dst):
        for j in range(4):
            block = pl.ds(128 * j, 128)
            p = (a[block, :].astype(F32) * b[block, :].astype(F32)).T
            for zt in range(8):
                dst[pl.ds(zt // 2 * 128 + zt % 2 * 4 + j, 16, stride=8), :] = p[16 * zt : 16 * zt + 16]

    copies[0].wait()
    copies[1].wait()
    product(first, value, tiles_g)
    pl.semaphore_wait(entry, 30)

    def to_plane(tiles, near, dq, which):
        base = rem(div(z, 2) + dq, 4) * 128
        here = rows(dq * 128 + yx * 8, 8)
        recv = r_xy.at[4 * which + dq]
        pltpu.make_async_copy(tiles.at[rows(base + yx * 8, 8)], near.at[here], recv).start()

        def step(there):
            remote(tiles.at[rows(base + there * 8, 8)], near.at[here], s_xy, recv, device(there, z, core)).start()

        plane(step)

    def pack(src, base, dst, to):
        for side in range(2):
            for j in range(4):
                dst[pl.ds(to + 64 * side + j, 16, stride=4), :] = src[pl.ds(base + 4 * side + j, 16, stride=8), :]

    def to_column(near, column, slots, dq, which):
        arrived(near.at[pl.ds(dq * 128, 128)], r_xy.at[4 * which + dq])
        pack(near, dq * 128, column, dq * 128)
        for side in range(2):
            zt = rem(div(z, 2) + dq, 4) * 2 + side
            src, dst, recv = column.at[pl.ds(dq * 128 + side * 64, 64)], slots.at[lands], r_z.at[8 * which + lands]
            if dq:
                remote(src, dst, s_z, recv, device(yx, zt, group)).start()
            else:
                send_or_keep(jnp.logical_and(zt == z, stays), src, dst, s_z, recv, device(yx, zt, group))

    order = (2, 1, 3, 0)
    for dq in order:
        to_plane(tiles_g, near_g, dq, 0)
    for c in copies[5:]:
        c.start()
    copies[4].wait()
    for j in range(4):
        block = pl.ds(128 * j, 128)
        taps_t[block, :] = taps[block, :].T
    across = rem(z + 4, 8)
    for j in range(4):
        taps_own[pl.ds(j, 16, stride=8), :] = taps_t[rows(128 * j + 16 * z, 16), :]
        taps_out[pl.ds(j, 16, stride=4), :] = taps_t[rows(128 * j + 16 * across, 16), :]
    remote(taps_out, taps_in, s_taps, r_taps, device(yx, across, core)).start()
    copies[2].wait()
    copies[3].wait()
    product(cot, gate, tiles_w)
    for dq in order:
        to_plane(tiles_w, near_w, dq, 1)
    for dq in order:
        to_column(near_g, column_g, slots_g, dq, 0)

    arrived(taps_in, r_taps)
    for j in range(4):
        taps_own[pl.ds(4 + j, 16, stride=8), :] = taps_in[pl.ds(j, 16, stride=4), :]

    def spread(src, dst, base, send, recv):
        here = rows(base + yx * 8, 8)
        pltpu.make_async_copy(src.at[here], dst.at[here], recv).start()

        def step(there):
            remote(src.at[rows(base + there * 8, 8)], dst.at[here], send, recv, device(there, z, core)).start()

        plane(step)

    spread(taps_own, taps_all, 0, s_txy, r_txy)
    for dq in order:
        to_column(near_w, column_w, slots_w, dq, 1)

    for c in copies[5:]:
        c.wait()
    cosine, sine = twiddle[0], twiddle[1]

    def side_by_side(parts):
        return jnp.concatenate(parts, axis=1) if len(parts) > 1 else parts[0]

    def stacked(parts):
        return jnp.concatenate(parts, axis=0) if len(parts) > 1 else parts[0]

    def forward(matrix, signals):
        a = left(matrix, side_by_side(signals))
        turned = []
        for i in range(len(signals)):
            re, im = a[:128, 128 * i : 128 * i + 128], a[128:, 128 * i : 128 * i + 128]
            turned.append(side_by_side([re * cosine + im * sine, im * cosine - re * sine]))
        f = right(stacked(turned), m_ahead)
        return [f[128 * i : 128 * i + 128] for i in range(len(signals))]

    def inverse(spectra_in):
        d = right(stacked([side_by_side(list(pair)) for pair in spectra_in]), m_back)
        turned = []
        for i in range(len(spectra_in)):
            dr, di = d[128 * i : 128 * i + 128, :128], d[128 * i : 128 * i + 128, 128:]
            turned.append(stacked([dr * cosine - di * sine, di * cosine + dr * sine]))
        y = left(m_finish, side_by_side(turned))
        return [y[:, 128 * i : 128 * i + 128] for i in range(len(spectra_in))]

    def signal(slots, bq, which):
        arrived(slots.at[bq], r_z.at[8 * which + bq])
        arrived(slots.at[4 + bq], r_z.at[8 * which + 4 + bq])
        return stacked([slots[bq], slots[4 + bq]])

    arrived(taps_all, r_txy)
    h = forward(m_taps.at[zh], [taps_all[...]])[0]
    hr, hi = h[:, :128], h[:, 128:]

    def turn(i):
        return rem(i + z, 4)

    def home(i):
        bq = turn(i)
        arrived(conv_in.at[pl.ds(128 * i, 128)], r_bxy.at[i])
        pack(conv_in, 128 * i, conv_pack, 128 * i)
        for side in range(2):
            z_to, core_to = 4 * side + 2 * core + div(bq, 2), rem(bq, 2)
            send_or_keep(
                jnp.logical_and(z_to == z, core_to == core),
                conv_pack.at[pl.ds(128 * i + 64 * side, 64)], conv_all.at[rows(64 * z, 64)],
                s_bz, r_bz, device(yx, z_to, core_to),
            )

    for first_i in range(0, 4, 2):
        group_i = range(first_i, first_i + 2)
        found = forward(m_signal, [signal(slots_g, turn(i), 0) for i in group_i])
        filtered = []
        for i, g in zip(group_i, found):
            spectra[i] = g
            gr, gi = g[:, :128], g[:, 128:]
            filtered.append((gr * hr - gi * hi, gr * hi + gi * hr))
        for i, result in zip(group_i, inverse(filtered)):
            conv[pl.ds(128 * i, 128), :] = result
            spread(conv, conv_in, 128 * i, s_bxy, r_bxy.at[i])

    total_re = total_im = 0.0
    for first_i in range(0, 4, 4):
        group_i = range(first_i, first_i + 4)
        for i, w in zip(group_i, forward(m_signal, [signal(slots_w, turn(i), 1) for i in group_i])):
            wr, wi = w[:, :128], w[:, 128:]
            gr, gi = spectra[i, :, :128], spectra[i, :, 128:]
            total_re = total_re + (wr * gr + wi * gi)
            total_im = total_im + (wi * gr - wr * gi)

    part[...] = inverse([(total_re, total_im)])[0]
    keeper = rem(z, 2) == core
    sibling = device(yx, z, 1 - core)

    @pl.when(jnp.logical_not(keeper))
    def _():
        remote(part, part_in, s_sib, r_sib, sibling).start()

    home(0)
    home(1)

    @pl.when(keeper)
    def _():
        arrived(part_in, r_sib)
        whole[...] = (part[...] + part_in[...]) * (1.0 / math.sqrt(8 * LENGTH))
        spread(whole, grad_in, 0, s_gxy, r_gxy)

    home(2)

    @pl.when(keeper)
    def _():
        arrived(grad_in, r_gxy)
        pack(grad_in, 0, grad_pack, 0)
        pltpu.make_async_copy(grad_pack.at[rows(64 * zh, 64)], grad_all.at[div(z, 2), core], r_gz).start()
        for dz in (4, 3, 5, 2, 6, 1, 7):
            zt = rem(z + dz, 8)
            remote(
                grad_pack.at[rows(64 * div(zt, 4), 64)], grad_all.at[div(z, 2), core], s_gz, r_gz, device(yx, zt, core)
            ).start()

    home(3)
    arrived(grad_all.at[:, core], r_gz)
    last = remote(grad_all.at[:, core], grad_all.at[:, core], s_last, r_last, sibling)
    last.start()
    for j in range(4):
        block, half = pl.ds(128 * j, 128), pl.ds(128 * (j % 2), 128)
        gated = first[block, :].astype(F32) * value[block, :].astype(F32)
        (direct_low, direct_high)[j // 2][half, :] = gate[block, :].astype(F32) * gated
    arrived(conv_all, r_bz)
    for j in range(4):
        block, half = pl.ds(128 * j, 128), pl.ds(128 * (j % 2), 128)
        c = conv_all[pl.ds(j, 128, stride=4), :].T
        (filtered_low, filtered_high)[j // 2][half, :] = gate[block, :].astype(F32) * c

    arrived(grad_all.at[:, 1 - core], r_last)
    flat = grad_all[...].reshape(512, 128)
    taps_t[...] = flat
    for j in range(4):
        (grad_low, grad_high)[j // 2][pl.ds(128 * (j % 2), 128), :] = taps_t[pl.ds(j, 128, stride=4), :].T

    last.wait_send()
    arrived(taps_out, s_taps)
    arrived(taps_own.at[pl.ds(0, 120)], s_txy)
    arrived(tiles_g.at[pl.ds(0, 480)], s_xy)
    arrived(tiles_w.at[pl.ds(0, 480)], s_xy)
    arrived(column_g.at[pl.ds(0, 448)], s_z)
    arrived(column_w.at[pl.ds(0, 448)], s_z)
    arrived(conv.at[pl.ds(0, 480)], s_bxy)
    arrived(conv_pack.at[pl.ds(0, 448)], s_bz)

    @pl.when(jnp.logical_not(stays))
    def _():
        arrived(column_w.at[pl.ds(0, 128)], s_z)
        arrived(conv_pack.at[pl.ds(0, 64)], s_bz)

    @pl.when(jnp.logical_not(keeper))
    def _():
        arrived(part, s_sib)

    @pl.when(keeper)
    def _():
        arrived(whole.at[pl.ds(0, 120)], s_gxy)
        arrived(conv.at[pl.ds(0, 448)], s_gz)


def combine(
    filtered_low, filtered_high, direct_low, direct_high, grad_low, grad_high, skip_h, out_h, grad_h, skip, out, sems
):
    get = pltpu.make_async_copy(skip_h, skip, sems.at[0])
    low = pltpu.make_async_copy(grad_low, grad_h.at[pl.ds(0, 256)], sems.at[1])
    high = pltpu.make_async_copy(grad_high, grad_h.at[pl.ds(256, 256)], sems.at[2])
    get.start()
    low.start()
    high.start()
    get.wait()
    out[pl.ds(0, 256), :] = (filtered_low[...] + skip[...] * direct_low[...]).astype(BF16)
    out[pl.ds(256, 256), :] = (filtered_high[...] + skip[...] * direct_high[...]).astype(BF16)
    put = pltpu.make_async_copy(out, out_h.at[0], sems.at[3])
    put.start()
    low.wait()
    high.wait()
    put.wait()


def shards(first_input, value_input, gate_input, cotangent, filter_taps, skip_weight):
    constants = tables()
    vmem, hbm = pl.BlockSpec(memory_space=pltpu.VMEM), pl.BlockSpec(memory_space=pltpu.HBM)
    dma = pltpu.SemaphoreType.DMA
    square, tall, short = (pltpu.VMEM((n, 128), F32) for n in (128, 512, 64))
    operands = [
        first_input, value_input, gate_input, cotangent, filter_taps,
        *[jnp.asarray(c) for c in constants],
    ]
    long = pltpu.VMEM((512, 128), BF16)
    half = jax.ShapeDtypeStruct((256, 128), F32)
    halves_out = pl.pallas_call(
        kernel,
        out_shape=(half,) * 6,
        in_specs=[hbm] * 11,
        out_specs=(vmem,) * 6,
        scratch_shapes=[
            long, long, long, long, tall, *[pltpu.VMEM(c.shape, c.dtype) for c in constants],
            tall, tall, tall, tall, tall, tall,
            pltpu.VMEM((8, 64, 128), F32), pltpu.VMEM((8, 64, 128), F32),
            tall, short, short, square, square,
            pltpu.VMEM((4, 128, 256), F32),
            tall, tall, tall, tall,
            square, square, square, square, square,
            pltpu.VMEM((4, 2, 64, 128), F32),
            dma((11,)), dma, dma, dma, dma, dma, dma((8,)), dma, dma((16,)), dma, dma((4,)), dma, dma,
            dma, dma, dma, dma, dma, dma, dma, dma,
        ],
        compiler_params=pltpu.CompilerParams(
            collective_id=1, has_side_effects=True, vmem_limit_bytes=55766016
        ),
        name="hyena",
    )(*operands)
    return pl.pallas_call(
        combine,
        out_shape=(
            jax.ShapeDtypeStruct((1, 512, 128), BF16),
            jax.ShapeDtypeStruct((512, 128), F32),
        ),
        in_specs=[vmem] * 6 + [hbm],
        out_specs=(hbm, hbm),
        scratch_shapes=[pltpu.VMEM((1, 128), F32), long, dma((4,))],
        compiler_params=pltpu.CompilerParams(vmem_limit_bytes=4 * 2**20),
        name="combine",
    )(*halves_out, skip_weight[None])


def solution(mesh):
    long, filt = P("dp", "seq", None), P("seq", None)
    return jax.shard_map(
        shards,
        mesh=mesh,
        in_specs=(long, long, long, long, filt, P()),
        out_specs=(long, filt),
        check_vma=False,
    )
```

```python
import functools
import math

import jax
import jax.numpy as jnp
import ml_dtypes
import numpy as np
from jax import lax
from jax.experimental import pallas as pl
from jax.experimental.pallas import tpu as pltpu
from jax.sharding import PartitionSpec as P

MESH = pl.DeviceIdType.MESH
F32 = jnp.float32
BF16 = jnp.bfloat16
LENGTH = 16384
PADDED = 2 * LENGTH


def halves(matrix):
    high = matrix.astype(ml_dtypes.bfloat16)
    low = (matrix - high.astype(np.float64)).astype(ml_dtypes.bfloat16)
    return np.stack([high, low])


def tables():
    freq = np.arange(128) + 0.5

    def outer(*axes):
        yx, zh, j = (a.reshape(-1) for a in np.broadcast_arrays(*axes))
        n1 = 8 * yx + 4 * zh + j
        phase = 2.0 * math.pi / 256.0 * ((n1[None, :] * freq[:, None]) % 256.0)
        return np.concatenate([np.cos(phase), -np.sin(phase)], axis=0)

    a16, a2, a4 = np.arange(16), np.arange(2), np.arange(4)
    signal = outer(a16[None, :, None], a2[:, None, None], a4)
    taps = [halves(outer(a16[:, None, None], a2[:, None] ^ own, a4)) for own in range(2)]
    turn = 2.0 * math.pi / PADDED * (np.arange(128)[None, :] * freq[:, None])
    twiddle = np.stack([np.cos(turn), np.sin(turn)]).astype(np.float32)
    inner = 2.0 * math.pi / 128.0 * (np.arange(128)[:, None] * np.arange(128)[None, :] % 128)
    cosine, sine = np.cos(inner), np.sin(inner)
    ahead = np.block([[cosine, -sine], [sine, cosine]])
    back = np.block([[cosine, sine], [-sine, cosine]])
    finish = outer(a16[:, None, None], a2[:, None], a4).T * (2.0 / PADDED)
    return halves(signal), np.stack(taps), halves(ahead), halves(back), halves(finish), twiddle


def split(x):
    high = x.astype(BF16)
    return high, (x - high.astype(F32)).astype(BF16)


def dot(a, b):
    return jnp.dot(a, b, preferred_element_type=F32)


def left(matrix, x):
    high, low = split(x)
    return dot(matrix[0], high) + (dot(matrix[0], low) + dot(matrix[1], high))


def right(x, matrix):
    high, low = split(x)
    return dot(high, matrix[0]) + (dot(low, matrix[0]) + dot(high, matrix[1]))


def kernel(
    first_h, value_h, gate_h, cot_h, taps_h, signal_h, taps_mh, ahead_h, back_h, finish_h, twiddle_h,
    filtered_low, filtered_high, direct_low, direct_high, grad_low, grad_high,
    first, value, gate, cot, taps, m_signal, m_taps, m_ahead, m_back, m_finish, twiddle,
    tiles_g, tiles_w, near_g, near_w, column_g, column_w, slots_g, slots_w,
    taps_t, taps_out, taps_in, taps_own, taps_all, spectra,
    conv, conv_in, conv_pack, conv_all, part, part_in, whole, grad_in, grad_pack, grad_all,
    loads, s_taps, r_taps, s_txy, r_txy, s_xy, r_xy, s_z, r_z, s_bxy, r_bxy, s_bz, r_bz,
    s_sib, r_sib, s_gxy, r_gxy, s_gz, r_gz, s_last, r_last,
):
    dp, seq = lax.axis_index("dp"), lax.axis_index("seq")
    div, rem = lax.div, lax.rem
    yx, zh, zl, core = div(seq, 2), rem(seq, 2), div(dp, 2), rem(dp, 2)
    z = zh * 4 + zl
    y, x = div(yx, 4), rem(yx, 4)
    group = div(zl, 2)
    stays = group == core
    lands = zh * 4 + rem(zl, 2) * 2 + core

    def device(yx_, z_, core_):
        return {"dp": rem(z_, 4) * 2 + core_, "seq": yx_ * 2 + div(z_, 4)}

    def beside(i):
        return rem(y + i // 4, 4) * 4 + rem(x + i % 4, 4)

    def plane(step):
        for i in range(1, 16):
            step(beside(i))

    def rows(start, count):
        return pl.ds(pl.multiple_of(start, 8), count)

    def remote(src, dst, send, recv, where):
        return pltpu.make_async_remote_copy(
            src_ref=src, dst_ref=dst, send_sem=send, recv_sem=recv, device_id=where, device_id_type=MESH
        )

    def arrived(ref, sem):
        pltpu.make_async_copy(ref, ref, sem).wait()

    def send_or_keep(mine, src, dst, send, recv, where):
        @pl.when(mine)
        def _():
            pltpu.make_async_copy(src, dst, recv).start()

        @pl.when(jnp.logical_not(mine))
        def _():
            remote(src, dst, send, recv, where).start()

    copies = [
        pltpu.make_async_copy(src, dst, loads.at[i])
        for i, (src, dst) in enumerate([
            (first_h.at[0], first), (value_h.at[0], value), (cot_h.at[0], cot), (gate_h.at[0], gate),
            (taps_h, taps), (signal_h, m_signal), (taps_mh, m_taps), (ahead_h, m_ahead),
            (back_h, m_back), (finish_h, m_finish), (twiddle_h, twiddle),
        ])
    ]
    for c in copies[:5]:
        c.start()

    entry = pltpu.get_barrier_semaphore()

    def greet(where):
        pl.semaphore_signal(entry, inc=1, device_id=where, device_id_type=MESH)

    for i in range(1, 16):
        other = rem(z * 2 + core + i, 16)
        greet(device(yx, div(other, 2), rem(other, 2)))
    plane(lambda there: greet(device(there, z, core)))

    def product(a, b, dst):
        for j in range(4):
            block = pl.ds(128 * j, 128)
            p = (a[block, :].astype(F32) * b[block, :].astype(F32)).T
            for zt in range(8):
                dst[pl.ds(zt // 2 * 128 + zt % 2 * 4 + j, 16, stride=8), :] = p[16 * zt : 16 * zt + 16]

    copies[0].wait()
    copies[1].wait()
    product(first, value, tiles_g)
    pl.semaphore_wait(entry, 30)

    def to_plane(tiles, near, dq, which):
        base = rem(div(z, 2) + dq, 4) * 128
        here = rows(dq * 128 + yx * 8, 8)
        recv = r_xy.at[4 * which + dq]
        pltpu.make_async_copy(tiles.at[rows(base + yx * 8, 8)], near.at[here], recv).start()

        def step(there):
            remote(tiles.at[rows(base + there * 8, 8)], near.at[here], s_xy, recv, device(there, z, core)).start()

        plane(step)

    def pack(src, base, dst, to):
        for side in range(2):
            for j in range(4):
                dst[pl.ds(to + 64 * side + j, 16, stride=4), :] = src[pl.ds(base + 4 * side + j, 16, stride=8), :]

    def to_column(near, column, slots, dq, which):
        arrived(near.at[pl.ds(dq * 128, 128)], r_xy.at[4 * which + dq])
        pack(near, dq * 128, column, dq * 128)
        for side in range(2):
            zt = rem(div(z, 2) + dq, 4) * 2 + side
            src, dst, recv = column.at[pl.ds(dq * 128 + side * 64, 64)], slots.at[lands], r_z.at[8 * which + lands]
            if dq:
                remote(src, dst, s_z, recv, device(yx, zt, group)).start()
            else:
                send_or_keep(jnp.logical_and(zt == z, stays), src, dst, s_z, recv, device(yx, zt, group))

    order = (2, 1, 3, 0)
    for dq in order:
        to_plane(tiles_g, near_g, dq, 0)
    copies[4].wait()
    for j in range(4):
        block = pl.ds(128 * j, 128)
        taps_t[block, :] = taps[block, :].T
    across = rem(z + 4, 8)
    for j in range(4):
        taps_own[pl.ds(j, 16, stride=8), :] = taps_t[rows(128 * j + 16 * z, 16), :]
        taps_out[pl.ds(j, 16, stride=4), :] = taps_t[rows(128 * j + 16 * across, 16), :]
    remote(taps_out, taps_in, s_taps, r_taps, device(yx, across, core)).start()
    copies[2].wait()
    copies[3].wait()
    product(cot, gate, tiles_w)
    for dq in order:
        to_column(near_g, column_g, slots_g, dq, 0)
        to_plane(tiles_w, near_w, dq, 1)
    for c in copies[5:]:
        c.start()

    arrived(taps_in, r_taps)
    for j in range(4):
        taps_own[pl.ds(4 + j, 16, stride=8), :] = taps_in[pl.ds(j, 16, stride=4), :]

    def spread(src, dst, base, send, recv):
        here = rows(base + yx * 8, 8)
        pltpu.make_async_copy(src.at[here], dst.at[here], recv).start()

        def step(there):
            remote(src.at[rows(base + there * 8, 8)], dst.at[here], send, recv, device(there, z, core)).start()

        plane(step)

    spread(taps_own, taps_all, 0, s_txy, r_txy)
    for dq in order:
        to_column(near_w, column_w, slots_w, dq, 1)

    for c in copies[5:]:
        c.wait()
    cosine, sine = twiddle[0], twiddle[1]

    def side_by_side(parts):
        return jnp.concatenate(parts, axis=1) if len(parts) > 1 else parts[0]

    def stacked(parts):
        return jnp.concatenate(parts, axis=0) if len(parts) > 1 else parts[0]

    def forward(matrix, signals):
        a = left(matrix, side_by_side(signals))
        turned = []
        for i in range(len(signals)):
            re, im = a[:128, 128 * i : 128 * i + 128], a[128:, 128 * i : 128 * i + 128]
            turned.append(side_by_side([re * cosine + im * sine, im * cosine - re * sine]))
        f = right(stacked(turned), m_ahead)
        return [f[128 * i : 128 * i + 128] for i in range(len(signals))]

    def inverse(spectra_in):
        d = right(stacked([side_by_side(list(pair)) for pair in spectra_in]), m_back)
        turned = []
        for i in range(len(spectra_in)):
            dr, di = d[128 * i : 128 * i + 128, :128], d[128 * i : 128 * i + 128, 128:]
            turned.append(stacked([dr * cosine - di * sine, di * cosine + dr * sine]))
        y = left(m_finish, side_by_side(turned))
        return [y[:, 128 * i : 128 * i + 128] for i in range(len(spectra_in))]

    def signal(slots, bq, which):
        arrived(slots.at[bq], r_z.at[8 * which + bq])
        arrived(slots.at[4 + bq], r_z.at[8 * which + 4 + bq])
        return stacked([slots[bq], slots[4 + bq]])

    arrived(taps_all, r_txy)
    h = forward(m_taps.at[zh], [taps_all[...]])[0]
    hr, hi = h[:, :128], h[:, 128:]

    def turn(i):
        return rem(i + z, 4)

    def home(i):
        bq = turn(i)
        arrived(conv_in.at[pl.ds(128 * i, 128)], r_bxy.at[i])
        pack(conv_in, 128 * i, conv_pack, 128 * i)
        for side in range(2):
            z_to, core_to = 4 * side + 2 * core + div(bq, 2), rem(bq, 2)
            send_or_keep(
                jnp.logical_and(z_to == z, core_to == core),
                conv_pack.at[pl.ds(128 * i + 64 * side, 64)], conv_all.at[rows(64 * z, 64)],
                s_bz, r_bz, device(yx, z_to, core_to),
            )

    for first_i in range(0, 4, 2):
        group_i = range(first_i, first_i + 2)
        found = forward(m_signal, [signal(slots_g, turn(i), 0) for i in group_i])
        filtered = []
        for i, g in zip(group_i, found):
            spectra[i] = g
            gr, gi = g[:, :128], g[:, 128:]
            filtered.append((gr * hr - gi * hi, gr * hi + gi * hr))
        for i, result in zip(group_i, inverse(filtered)):
            conv[pl.ds(128 * i, 128), :] = result
            spread(conv, conv_in, 128 * i, s_bxy, r_bxy.at[i])

    total_re = total_im = 0.0
    for first_i in range(0, 4, 4):
        group_i = range(first_i, first_i + 4)
        for i, w in zip(group_i, forward(m_signal, [signal(slots_w, turn(i), 1) for i in group_i])):
            wr, wi = w[:, :128], w[:, 128:]
            gr, gi = spectra[i, :, :128], spectra[i, :, 128:]
            total_re = total_re + (wr * gr + wi * gi)
            total_im = total_im + (wi * gr - wr * gi)

    part[...] = inverse([(total_re, total_im)])[0]
    keeper = rem(z, 2) == core
    sibling = device(yx, z, 1 - core)

    @pl.when(jnp.logical_not(keeper))
    def _():
        remote(part, part_in, s_sib, r_sib, sibling).start()

    home(0)
    home(1)

    @pl.when(keeper)
    def _():
        arrived(part_in, r_sib)
        whole[...] = (part[...] + part_in[...]) * (1.0 / math.sqrt(8 * LENGTH))
        spread(whole, grad_in, 0, s_gxy, r_gxy)

    home(2)

    @pl.when(keeper)
    def _():
        arrived(grad_in, r_gxy)
        pack(grad_in, 0, grad_pack, 0)
        pltpu.make_async_copy(grad_pack.at[rows(64 * zh, 64)], grad_all.at[div(z, 2), core], r_gz.at[div(z, 2)]).start()
        for dz in (4, 3, 5, 2, 6, 1, 7):
            zt = rem(z + dz, 8)
            remote(
                grad_pack.at[rows(64 * div(zt, 4), 64)], grad_all.at[div(z, 2), core], s_gz, r_gz.at[div(z, 2)], device(yx, zt, core)
            ).start()

    home(3)
    for d in (0, 1, 3, 2):
        block = grad_all.at[rem(div(z, 2) + d, 4), core]
        arrived(block, r_gz.at[rem(div(z, 2) + d, 4)])
        remote(block, block, s_last, r_last, sibling).start()
    for j in range(4):
        block, half = pl.ds(128 * j, 128), pl.ds(128 * (j % 2), 128)
        gated = first[block, :].astype(F32) * value[block, :].astype(F32)
        (direct_low, direct_high)[j // 2][half, :] = gate[block, :].astype(F32) * gated
    arrived(conv_all, r_bz)
    for j in range(4):
        block, half = pl.ds(128 * j, 128), pl.ds(128 * (j % 2), 128)
        c = conv_all[pl.ds(j, 128, stride=4), :].T
        (filtered_low, filtered_high)[j // 2][half, :] = gate[block, :].astype(F32) * c

    arrived(grad_all.at[:, 1 - core], r_last)
    flat = grad_all[...].reshape(512, 128)
    taps_t[...] = flat
    for j in range(4):
        (grad_low, grad_high)[j // 2][pl.ds(128 * (j % 2), 128), :] = taps_t[pl.ds(j, 128, stride=4), :].T

    arrived(grad_all.at[:, core], s_last)
    arrived(taps_out, s_taps)
    arrived(taps_own.at[pl.ds(0, 120)], s_txy)
    arrived(tiles_g.at[pl.ds(0, 480)], s_xy)
    arrived(tiles_w.at[pl.ds(0, 480)], s_xy)
    arrived(column_g.at[pl.ds(0, 448)], s_z)
    arrived(column_w.at[pl.ds(0, 448)], s_z)
    arrived(conv.at[pl.ds(0, 480)], s_bxy)
    arrived(conv_pack.at[pl.ds(0, 448)], s_bz)

    @pl.when(jnp.logical_not(stays))
    def _():
        arrived(column_w.at[pl.ds(0, 128)], s_z)
        arrived(conv_pack.at[pl.ds(0, 64)], s_bz)

    @pl.when(jnp.logical_not(keeper))
    def _():
        arrived(part, s_sib)

    @pl.when(keeper)
    def _():
        arrived(whole.at[pl.ds(0, 120)], s_gxy)
        arrived(conv.at[pl.ds(0, 448)], s_gz)


def combine(
    filtered_low, filtered_high, direct_low, direct_high, grad_low, grad_high, skip_h, out_h, grad_h, skip, out, sems
):
    get = pltpu.make_async_copy(skip_h, skip, sems.at[0])
    low = pltpu.make_async_copy(grad_low, grad_h.at[pl.ds(0, 256)], sems.at[1])
    high = pltpu.make_async_copy(grad_high, grad_h.at[pl.ds(256, 256)], sems.at[2])
    get.start()
    low.start()
    high.start()
    get.wait()
    out[pl.ds(0, 256), :] = (filtered_low[...] + skip[...] * direct_low[...]).astype(BF16)
    out[pl.ds(256, 256), :] = (filtered_high[...] + skip[...] * direct_high[...]).astype(BF16)
    put = pltpu.make_async_copy(out, out_h.at[0], sems.at[3])
    put.start()
    low.wait()
    high.wait()
    put.wait()


def shards(first_input, value_input, gate_input, cotangent, filter_taps, skip_weight):
    constants = tables()
    vmem, hbm = pl.BlockSpec(memory_space=pltpu.VMEM), pl.BlockSpec(memory_space=pltpu.HBM)
    dma = pltpu.SemaphoreType.DMA
    square, tall, short = (pltpu.VMEM((n, 128), F32) for n in (128, 512, 64))
    operands = [
        first_input, value_input, gate_input, cotangent, filter_taps,
        *[jnp.asarray(c) for c in constants],
    ]
    long = pltpu.VMEM((512, 128), BF16)
    half = jax.ShapeDtypeStruct((256, 128), F32)
    halves_out = pl.pallas_call(
        kernel,
        out_shape=(half,) * 6,
        in_specs=[hbm] * 11,
        out_specs=(vmem,) * 6,
        scratch_shapes=[
            long, long, long, long, tall, *[pltpu.VMEM(c.shape, c.dtype) for c in constants],
            tall, tall, tall, tall, tall, tall,
            pltpu.VMEM((8, 64, 128), F32), pltpu.VMEM((8, 64, 128), F32),
            tall, short, short, square, square,
            pltpu.VMEM((4, 128, 256), F32),
            tall, tall, tall, tall,
            square, square, square, square, square,
            pltpu.VMEM((4, 2, 64, 128), F32),
            dma((11,)), dma, dma, dma, dma, dma, dma((8,)), dma, dma((16,)), dma, dma((4,)), dma, dma,
            dma, dma, dma, dma, dma, dma((4,)), dma, dma,
        ],
        compiler_params=pltpu.CompilerParams(
            collective_id=1, has_side_effects=True, vmem_limit_bytes=55766016
        ),
        name="hyena",
    )(*operands)
    return pl.pallas_call(
        combine,
        out_shape=(
            jax.ShapeDtypeStruct((1, 512, 128), BF16),
            jax.ShapeDtypeStruct((512, 128), F32),
        ),
        in_specs=[vmem] * 6 + [hbm],
        out_specs=(hbm, hbm),
        scratch_shapes=[pltpu.VMEM((1, 128), F32), long, dma((4,))],
        compiler_params=pltpu.CompilerParams(vmem_limit_bytes=4 * 2**20),
        name="combine",
    )(*halves_out, skip_weight[None])


def solution(mesh):
    long, filt = P("dp", "seq", None), P("seq", None)
    return jax.shard_map(
        shards,
        mesh=mesh,
        in_specs=(long, long, long, long, filt, P()),
        out_specs=(long, filt),
        check_vma=False,
    )
```

```python
import functools
import math

import jax
import jax.numpy as jnp
import ml_dtypes
import numpy as np
from jax import lax
from jax.experimental import pallas as pl
from jax.experimental.pallas import tpu as pltpu
from jax.sharding import PartitionSpec as P

MESH = pl.DeviceIdType.MESH
F32 = jnp.float32
BF16 = jnp.bfloat16
LENGTH = 16384
PADDED = 2 * LENGTH


def halves(matrix):
    high = matrix.astype(ml_dtypes.bfloat16)
    low = (matrix - high.astype(np.float64)).astype(ml_dtypes.bfloat16)
    return np.stack([high, low])


def tables():
    freq = np.arange(128) + 0.5

    def outer(*axes):
        yx, zh, j = (a.reshape(-1) for a in np.broadcast_arrays(*axes))
        n1 = 8 * yx + 4 * zh + j
        phase = 2.0 * math.pi / 256.0 * ((n1[None, :] * freq[:, None]) % 256.0)
        return np.concatenate([np.cos(phase), -np.sin(phase)], axis=0)

    a16, a2, a4 = np.arange(16), np.arange(2), np.arange(4)
    signal = outer(a16[None, :, None], a2[:, None, None], a4)
    taps = [halves(outer(a16[:, None, None], a2[:, None] ^ own, a4)) for own in range(2)]
    turn = 2.0 * math.pi / PADDED * (np.arange(128)[None, :] * freq[:, None])
    twiddle = np.stack([np.cos(turn), np.sin(turn)]).astype(np.float32)
    inner = 2.0 * math.pi / 128.0 * (np.arange(128)[:, None] * np.arange(128)[None, :] % 128)
    cosine, sine = np.cos(inner), np.sin(inner)
    ahead = np.block([[cosine, -sine], [sine, cosine]])
    back = np.block([[cosine, sine], [-sine, cosine]])
    finish = outer(a16[:, None, None], a2[:, None], a4).T * (2.0 / PADDED)
    return halves(signal), np.stack(taps), halves(ahead), halves(back), halves(finish), twiddle


def split(x):
    high = x.astype(BF16)
    return high, (x - high.astype(F32)).astype(BF16)


def dot(a, b):
    return jnp.dot(a, b, preferred_element_type=F32)


def left(matrix, x):
    high, low = split(x)
    return dot(matrix[0], high) + (dot(matrix[0], low) + dot(matrix[1], high))


def right(x, matrix):
    high, low = split(x)
    return dot(high, matrix[0]) + (dot(low, matrix[0]) + dot(high, matrix[1]))


def kernel(
    first_h, value_h, gate_h, cot_h, taps_h, signal_h, taps_mh, ahead_h, back_h, finish_h, twiddle_h,
    filtered_low, filtered_high, direct_low, direct_high, grad_low, grad_high,
    first, value, gate, cot, taps, m_signal, m_taps, m_ahead, m_back, m_finish, twiddle,
    tiles_g, tiles_w, near_g, near_w, column_g, column_w, slots_g, slots_w,
    taps_t, taps_out, taps_in, taps_own, taps_all, spectra,
    conv, conv_in, conv_pack, conv_all, part, part_in, whole, grad_in, grad_pack, grad_all,
    loads, s_taps, r_taps, s_txy, r_txy, s_xy, r_xy, s_z, r_z, s_bxy, r_bxy, s_bz, r_bz,
    s_sib, r_sib, s_gxy, r_gxy, s_gz, r_gz, s_last, r_last,
):
    dp, seq = lax.axis_index("dp"), lax.axis_index("seq")
    div, rem = lax.div, lax.rem
    yx, zh, zl, core = div(seq, 2), rem(seq, 2), div(dp, 2), rem(dp, 2)
    z = zh * 4 + zl
    y, x = div(yx, 4), rem(yx, 4)
    group = div(zl, 2)
    stays = group == core
    lands = zh * 4 + rem(zl, 2) * 2 + core

    def device(yx_, z_, core_):
        return {"dp": rem(z_, 4) * 2 + core_, "seq": yx_ * 2 + div(z_, 4)}

    def beside(i):
        return rem(y + i // 4, 4) * 4 + rem(x + i % 4, 4)

    def plane(step):
        for i in range(1, 16):
            step(beside(i))

    def rows(start, count):
        return pl.ds(pl.multiple_of(start, 8), count)

    def remote(src, dst, send, recv, where):
        return pltpu.make_async_remote_copy(
            src_ref=src, dst_ref=dst, send_sem=send, recv_sem=recv, device_id=where, device_id_type=MESH
        )

    def arrived(ref, sem):
        pltpu.make_async_copy(ref, ref, sem).wait()

    def send_or_keep(mine, src, dst, send, recv, where):
        @pl.when(mine)
        def _():
            pltpu.make_async_copy(src, dst, recv).start()

        @pl.when(jnp.logical_not(mine))
        def _():
            remote(src, dst, send, recv, where).start()

    copies = [
        pltpu.make_async_copy(src, dst, loads.at[i])
        for i, (src, dst) in enumerate([
            (first_h.at[0], first), (value_h.at[0], value), (cot_h.at[0], cot), (gate_h.at[0], gate),
            (taps_h, taps), (signal_h, m_signal), (taps_mh, m_taps), (ahead_h, m_ahead),
            (back_h, m_back), (finish_h, m_finish), (twiddle_h, twiddle),
        ])
    ]
    for c in copies[:5]:
        c.start()

    entry = pltpu.get_barrier_semaphore()

    def greet(where):
        pl.semaphore_signal(entry, inc=1, device_id=where, device_id_type=MESH)

    for i in range(1, 16):
        other = rem(z * 2 + core + i, 16)
        greet(device(yx, div(other, 2), rem(other, 2)))
    plane(lambda there: greet(device(there, z, core)))

    def product(a, b, dst):
        for j in range(4):
            block = pl.ds(128 * j, 128)
            p = (a[block, :].astype(F32) * b[block, :].astype(F32)).T
            for zt in range(8):
                place = pl.ds(zt % 2 * 4 + j, 16, stride=8)
                dst[zt // 2, place, :] = p[16 * zt : 16 * zt + 16]

    copies[0].wait()
    copies[1].wait()
    product(first, value, tiles_g)
    pl.semaphore_wait(entry, 30)

    def to_plane(tiles, near, dq, which):
        base = rem(div(z, 2) + dq, 4)
        here = rows(dq * 128 + yx * 8, 8)
        recv = r_xy.at[4 * which + dq]
        pltpu.make_async_copy(tiles.at[base, rows(yx * 8, 8)], near.at[here], recv).start()

        def step(there):
            remote(tiles.at[base, rows(there * 8, 8)], near.at[here], s_xy, recv, device(there, z, core)).start()

        plane(step)

    def all_to_plane():
        here = near_w.at[:, rows(yx * 8, 8)]
        pltpu.make_async_copy(tiles_w.at[:, rows(yx * 8, 8)], here, r_xy.at[4]).start()

        def step(there):
            remote(tiles_w.at[:, rows(there * 8, 8)], here, s_xy, r_xy.at[4], device(there, z, core)).start()

        plane(step)

    def pack(src, base, dst, to):
        for side in range(2):
            for j in range(4):
                dst[pl.ds(to + 64 * side + j, 16, stride=4), :] = src[pl.ds(base + 4 * side + j, 16, stride=8), :]

    def to_column(near, column, slots, dq, which):
        if which:
            pack(near.at[rem(div(z, 2) + dq, 4)], 0, column, dq * 128)
        else:
            arrived(near.at[pl.ds(dq * 128, 128)], r_xy.at[dq])
            pack(near, dq * 128, column, dq * 128)
        for side in range(2):
            zt = rem(div(z, 2) + dq, 4) * 2 + side
            src, dst, recv = column.at[pl.ds(dq * 128 + side * 64, 64)], slots.at[lands], r_z.at[8 * which + lands]
            if dq:
                remote(src, dst, s_z, recv, device(yx, zt, group)).start()
            else:
                send_or_keep(jnp.logical_and(zt == z, stays), src, dst, s_z, recv, device(yx, zt, group))

    order = (2, 3, 1, 0)
    for dq in order:
        to_plane(tiles_g, near_g, dq, 0)
    copies[4].wait()
    for j in range(4):
        block = pl.ds(128 * j, 128)
        taps_t[block, :] = taps[block, :].T
    across = rem(z + 4, 8)
    for j in range(4):
        taps_own[pl.ds(j, 16, stride=8), :] = taps_t[rows(128 * j + 16 * z, 16), :]
        taps_out[pl.ds(j, 16, stride=4), :] = taps_t[rows(128 * j + 16 * across, 16), :]
    remote(taps_out, taps_in, s_taps, r_taps, device(yx, across, core)).start()
    copies[2].wait()
    copies[3].wait()
    product(cot, gate, tiles_w)
    for dq in order:
        to_column(near_g, column_g, slots_g, dq, 0)
        if dq == order[0]:
            all_to_plane()
    for c in copies[5:]:
        c.start()

    arrived(taps_in, r_taps)
    for j in range(4):
        taps_own[pl.ds(4 + j, 16, stride=8), :] = taps_in[pl.ds(j, 16, stride=4), :]

    def spread(src, dst, base, send, recv):
        here = rows(base + yx * 8, 8)
        pltpu.make_async_copy(src.at[here], dst.at[here], recv).start()

        def step(there):
            remote(src.at[rows(base + there * 8, 8)], dst.at[here], send, recv, device(there, z, core)).start()

        plane(step)

    spread(taps_own, taps_all, 0, s_txy, r_txy)
    arrived(near_w, r_xy.at[4])
    for dq in order:
        to_column(near_w, column_w, slots_w, dq, 1)

    for c in copies[5:]:
        c.wait()
    cosine, sine = twiddle[0], twiddle[1]

    def side_by_side(parts):
        return jnp.concatenate(parts, axis=1) if len(parts) > 1 else parts[0]

    def stacked(parts):
        return jnp.concatenate(parts, axis=0) if len(parts) > 1 else parts[0]

    def forward(matrix, signals):
        a = left(matrix, side_by_side(signals))
        turned = []
        for i in range(len(signals)):
            re, im = a[:128, 128 * i : 128 * i + 128], a[128:, 128 * i : 128 * i + 128]
            turned.append(side_by_side([re * cosine + im * sine, im * cosine - re * sine]))
        f = right(stacked(turned), m_ahead)
        return [f[128 * i : 128 * i + 128] for i in range(len(signals))]

    def inverse(spectra_in):
        d = right(stacked([side_by_side(list(pair)) for pair in spectra_in]), m_back)
        turned = []
        for i in range(len(spectra_in)):
            dr, di = d[128 * i : 128 * i + 128, :128], d[128 * i : 128 * i + 128, 128:]
            turned.append(stacked([dr * cosine - di * sine, di * cosine + dr * sine]))
        y = left(m_finish, side_by_side(turned))
        return [y[:, 128 * i : 128 * i + 128] for i in range(len(spectra_in))]

    def signal(slots, bq, which):
        arrived(slots.at[bq], r_z.at[8 * which + bq])
        arrived(slots.at[4 + bq], r_z.at[8 * which + 4 + bq])
        return stacked([slots[bq], slots[4 + bq]])

    arrived(taps_all, r_txy)
    h = forward(m_taps.at[zh], [taps_all[...]])[0]
    hr, hi = h[:, :128], h[:, 128:]

    def turn(i):
        return rem(i + z, 4)

    def home(i):
        bq = turn(i)
        arrived(conv_in.at[pl.ds(128 * i, 128)], r_bxy.at[i])
        pack(conv_in, 128 * i, conv_pack, 128 * i)
        for side in range(2):
            z_to, core_to = 4 * side + 2 * core + div(bq, 2), rem(bq, 2)
            send_or_keep(
                jnp.logical_and(z_to == z, core_to == core),
                conv_pack.at[pl.ds(128 * i + 64 * side, 64)], conv_all.at[rows(64 * z, 64)],
                s_bz, r_bz, device(yx, z_to, core_to),
            )

    for first_i in range(0, 4, 2):
        group_i = range(first_i, first_i + 2)
        found = forward(m_signal, [signal(slots_g, turn(i), 0) for i in group_i])
        filtered = []
        for i, g in zip(group_i, found):
            spectra[i] = g
            gr, gi = g[:, :128], g[:, 128:]
            filtered.append((gr * hr - gi * hi, gr * hi + gi * hr))
        for i, result in zip(group_i, inverse(filtered)):
            conv[pl.ds(128 * i, 128), :] = result
            spread(conv, conv_in, 128 * i, s_bxy, r_bxy.at[i])

    total_re = total_im = 0.0
    for first_i in range(0, 4, 4):
        group_i = range(first_i, first_i + 4)
        for i, w in zip(group_i, forward(m_signal, [signal(slots_w, turn(i), 1) for i in group_i])):
            wr, wi = w[:, :128], w[:, 128:]
            gr, gi = spectra[i, :, :128], spectra[i, :, 128:]
            total_re = total_re + (wr * gr + wi * gi)
            total_im = total_im + (wi * gr - wr * gi)

    part[...] = inverse([(total_re, total_im)])[0]
    keeper = rem(z, 2) == core
    sibling = device(yx, z, 1 - core)

    @pl.when(jnp.logical_not(keeper))
    def _():
        remote(part, part_in, s_sib, r_sib, sibling).start()

    home(0)
    home(1)

    @pl.when(keeper)
    def _():
        arrived(part_in, r_sib)
        whole[...] = (part[...] + part_in[...]) * (1.0 / math.sqrt(8 * LENGTH))
        spread(whole, grad_in, 0, s_gxy, r_gxy)

    home(2)

    @pl.when(keeper)
    def _():
        arrived(grad_in, r_gxy)
        pack(grad_in, 0, grad_pack, 0)
        pltpu.make_async_copy(grad_pack.at[rows(64 * zh, 64)], grad_all.at[div(z, 2), core], r_gz.at[div(z, 2)]).start()
        for dz in (4, 3, 5, 2, 6, 1, 7):
            zt = rem(z + dz, 8)
            remote(
                grad_pack.at[rows(64 * div(zt, 4), 64)], grad_all.at[div(z, 2), core], s_gz, r_gz.at[div(z, 2)], device(yx, zt, core)
            ).start()

    home(3)
    for d in (0, 1, 3, 2):
        block = grad_all.at[rem(div(z, 2) + d, 4), core]
        arrived(block, r_gz.at[rem(div(z, 2) + d, 4)])
        remote(block, block, s_last, r_last, sibling).start()
    for j in range(4):
        block, half = pl.ds(128 * j, 128), pl.ds(128 * (j % 2), 128)
        gated = first[block, :].astype(F32) * value[block, :].astype(F32)
        (direct_low, direct_high)[j // 2][half, :] = gate[block, :].astype(F32) * gated
    arrived(conv_all, r_bz)
    for j in range(4):
        block, half = pl.ds(128 * j, 128), pl.ds(128 * (j % 2), 128)
        c = conv_all[pl.ds(j, 128, stride=4), :].T
        (filtered_low, filtered_high)[j // 2][half, :] = gate[block, :].astype(F32) * c

    arrived(grad_all.at[:, 1 - core], r_last)
    flat = grad_all[...].reshape(512, 128)
    taps_t[...] = flat
    for j in range(4):
        (grad_low, grad_high)[j // 2][pl.ds(128 * (j % 2), 128), :] = taps_t[pl.ds(j, 128, stride=4), :].T

    arrived(grad_all.at[:, core], s_last)
    arrived(taps_out, s_taps)
    arrived(taps_own.at[pl.ds(0, 120)], s_txy)
    arrived(tiles_g.at[:, pl.ds(0, 120)], s_xy)
    arrived(tiles_w.at[:, pl.ds(0, 120)], s_xy)
    arrived(column_g.at[pl.ds(0, 448)], s_z)
    arrived(column_w.at[pl.ds(0, 448)], s_z)
    arrived(conv.at[pl.ds(0, 480)], s_bxy)
    arrived(conv_pack.at[pl.ds(0, 448)], s_bz)

    @pl.when(jnp.logical_not(stays))
    def _():
        arrived(column_w.at[pl.ds(0, 128)], s_z)
        arrived(conv_pack.at[pl.ds(0, 64)], s_bz)

    @pl.when(jnp.logical_not(keeper))
    def _():
        arrived(part, s_sib)

    @pl.when(keeper)
    def _():
        arrived(whole.at[pl.ds(0, 120)], s_gxy)
        arrived(conv.at[pl.ds(0, 448)], s_gz)


def combine(
    filtered_low, filtered_high, direct_low, direct_high, grad_low, grad_high, skip_h, out_h, grad_h, skip, out, sems
):
    get = pltpu.make_async_copy(skip_h, skip, sems.at[0])
    low = pltpu.make_async_copy(grad_low, grad_h.at[pl.ds(0, 256)], sems.at[1])
    high = pltpu.make_async_copy(grad_high, grad_h.at[pl.ds(256, 256)], sems.at[2])
    get.start()
    low.start()
    high.start()
    get.wait()
    out[pl.ds(0, 256), :] = (filtered_low[...] + skip[...] * direct_low[...]).astype(BF16)
    out[pl.ds(256, 256), :] = (filtered_high[...] + skip[...] * direct_high[...]).astype(BF16)
    put = pltpu.make_async_copy(out, out_h.at[0], sems.at[3])
    put.start()
    low.wait()
    high.wait()
    put.wait()


def shards(first_input, value_input, gate_input, cotangent, filter_taps, skip_weight):
    constants = tables()
    vmem, hbm = pl.BlockSpec(memory_space=pltpu.VMEM), pl.BlockSpec(memory_space=pltpu.HBM)
    dma = pltpu.SemaphoreType.DMA
    square, tall, short = (pltpu.VMEM((n, 128), F32) for n in (128, 512, 64))
    operands = [
        first_input, value_input, gate_input, cotangent, filter_taps,
        *[jnp.asarray(c) for c in constants],
    ]
    long = pltpu.VMEM((512, 128), BF16)
    quad = pltpu.VMEM((4, 128, 128), F32)
    half = jax.ShapeDtypeStruct((256, 128), F32)
    halves_out = pl.pallas_call(
        kernel,
        out_shape=(half,) * 6,
        in_specs=[hbm] * 11,
        out_specs=(vmem,) * 6,
        scratch_shapes=[
            long, long, long, long, tall, *[pltpu.VMEM(c.shape, c.dtype) for c in constants],
            quad, quad, tall, quad, tall, tall,
            pltpu.VMEM((8, 64, 128), F32), pltpu.VMEM((8, 64, 128), F32),
            tall, short, short, square, square,
            pltpu.VMEM((4, 128, 256), F32),
            tall, tall, tall, tall,
            square, square, square, square, square,
            pltpu.VMEM((4, 2, 64, 128), F32),
            dma((11,)), dma, dma, dma, dma, dma, dma((8,)), dma, dma((16,)), dma, dma((4,)), dma, dma,
            dma, dma, dma, dma, dma, dma((4,)), dma, dma,
        ],
        compiler_params=pltpu.CompilerParams(
            collective_id=1, has_side_effects=True, vmem_limit_bytes=55766016
        ),
        name="hyena",
    )(*operands)
    return pl.pallas_call(
        combine,
        out_shape=(
            jax.ShapeDtypeStruct((1, 512, 128), BF16),
            jax.ShapeDtypeStruct((512, 128), F32),
        ),
        in_specs=[vmem] * 6 + [hbm],
        out_specs=(hbm, hbm),
        scratch_shapes=[pltpu.VMEM((1, 128), F32), long, dma((4,))],
        compiler_params=pltpu.CompilerParams(vmem_limit_bytes=4 * 2**20),
        name="combine",
    )(*halves_out, skip_weight[None])


def solution(mesh):
    long, filt = P("dp", "seq", None), P("seq", None)
    return jax.shard_map(
        shards,
        mesh=mesh,
        in_specs=(long, long, long, long, filt, P()),
        out_specs=(long, filt),
        check_vma=False,
    )
```
